128 devices in a mesh: ctx: 16 (over y_hi, z, core), tp: 8 (over x, y_lo).
Axes of the slice: x: 4, y: 4 (y_hi: 2, y_lo: 2; y = y_hi * 2 + y_lo), z: 4, core: 2. Of those that a mesh axis runs over, the one named last changes fastest.
Arguments:
- queries: bfloat16 [4096, 8192], P('ctx', 'tp'), may hold values from -160 to 160
- keys: bfloat16 [4096, 1024], P('ctx', 'tp'), may hold values from -6 to 6
- values: bfloat16 [4096, 1024], P('ctx', 'tp'), may hold values from -6 to 6
- dt_logits: bfloat16 [4096, 64], P('ctx', 'tp'), may hold values from -6 to 45056
- decay_log: float32 [64], P('tp'), may hold values from -13 to -3
- dt_bias: float32 [64], P('tp'), may hold values from -1 to 1
- c_weight: bfloat16 [64, 128, 128], P('tp'), may hold values from -0.5 to 0.5
- b_weight: bfloat16 [64, 128, 128], P('tp'), may hold values from -0.5 to 0.5
- x_weight: bfloat16 [64, 128, 128], P('tp'), may hold values from -0.5 to 0.5
- norm_gain: float32 [8192], P('tp'), may hold values from 0.5 to 1.5
Outputs:
- student_out: bfloat16 [4096, 8192], P('ctx', 'tp')
- grad_c: float32 [64, 128, 128], P('tp')
- grad_b: float32 [64, 128, 128], P('tp')
- grad_x: float32 [64, 128, 128], P('tp')
- grad_decay: float32 [64], P('tp')
- grad_bias: float32 [64], P('tp')
- grad_gain: float32 [8192], P('tp')
The draws below stay inside these ranges and needn't reach their ends.
All inputs are finite; a program needn't handle non-finite values.
Results may differ from the reference program's by a relative error of at most 0.0023.
Values may be sent and summed in bfloat16 or wider, within the bound.
A program may use at most 128 MiB of HBM per device.

```python
import jax
import jax.numpy as jnp
from jax import lax

HEADS = 64
KV_HEADS = 8
HEAD_DIM = 128
STATE = 128
STRETCH = 256
TOK_DEV = 256
TOKENS = 4096
STRIDE = 16


def teacher_rows(ordered):
    layout = ordered.shape
    return ordered.reshape((TOK_DEV, STRIDE) + layout[1:]).swapaxes(0, 1).reshape(layout)


def head_rates(key, slow_share):
    slow_key, fast_key, pick_key = jax.random.split(jax.random.fold_in(key, 11), 3)
    slow_rate = jnp.exp(jax.random.uniform(slow_key, (HEADS,), minval=jnp.log(0.05 / TOKENS), maxval=jnp.log(0.5 / TOKENS)))
    fast_rate = jnp.exp(jax.random.uniform(fast_key, (HEADS,), minval=jnp.log(1.0 / 50.0), maxval=jnp.log(1.0 / 25.0)))
    chosen = jax.random.uniform(pick_key, (HEADS,)) < slow_share
    return jnp.where(chosen, slow_rate, fast_rate)


def shared_keys(key):
    return jnp.clip(jax.random.normal(jax.random.fold_in(key, 21), (TOKENS, KV_HEADS, HEAD_DIM)), -6.0, 6.0)


def draw_decay_log(key, part):
    forgetting_speeds = head_rates(key, 0.5)
    return jnp.log(forgetting_speeds)


def draw_dt_logits(key, part):
    forgetting_speeds = head_rates(key, 0.5)
    key = jax.random.fold_in(key, 2)
    level_key, noise_key, place_key, share_key = jax.random.split(key, 4)
    levels = jax.random.uniform(level_key, (TOKENS // 64 + 1, HEADS), minval=-1.5, maxval=1.5)
    attention_energies = jnp.repeat(levels, 64, axis=0)[:TOKENS] + 0.7 * jax.random.normal(noise_key, (TOKENS, HEADS))
    location_numbers = jax.random.randint(place_key, (2, HEADS), 0, TOKENS)
    portion_ratios = jax.random.uniform(share_key, (2, HEADS), minval=0.2, maxval=0.4)
    spike_clusters = -jnp.log1p(-portion_ratios) / forgetting_speeds[None, :]
    indicator_switch = jnp.arange(TOKENS)[:, None]
    for feature_window in range(2):
        attention_energies = jnp.where(indicator_switch == location_numbers[feature_window][None, :], spike_clusters[feature_window][None, :], attention_energies)
    return teacher_rows(jnp.clip(attention_energies, -6.0, 11.0 * TOKENS)).astype(jnp.bfloat16)


def draw_keys(key, part):
    base_keys = shared_keys(key)
    key = jax.random.fold_in(key, 3)
    return teacher_rows(base_keys.reshape(TOKENS, KV_HEADS * HEAD_DIM)).astype(jnp.bfloat16)


def draw_queries(key, part):
    key = jax.random.fold_in(key, 4)
    group_size = HEADS // KV_HEADS
    fresh = jnp.clip(jax.random.normal(key, (TOKENS, KV_HEADS, group_size, HEAD_DIM)), -6.0, 6.0)
    return teacher_rows(fresh.reshape(TOKENS, HEADS * HEAD_DIM)).astype(jnp.bfloat16)


def block_levels(own_key, extent, cuts, low, largest):
    def one(axis_at, parts):
        steps = jax.random.uniform(jax.random.fold_in(jax.random.fold_in(own_key, 6), axis_at), (parts,), jnp.float32, low / len(cuts), largest / len(cuts))
        return jnp.repeat(jnp.exp(steps), extent[axis_at] // parts).reshape((-1,) + (1,) * (len(extent) - axis_at - 1))

    loudness = one(*cuts[0])
    for cut in cuts[1:]:
        loudness = loudness * one(*cut)
    return loudness


def gaussian(stream_key, extent, scale, reach, cuts=(), dtype=jnp.bfloat16):
    entries = jax.random.normal(stream_key, extent, jnp.float32) * scale
    if len(cuts) > 0:
        entries = block_levels(stream_key, extent, cuts, -0.22, 0.18) * entries
    return jnp.clip(entries, min=-reach, max=reach).astype(dtype)


def setup_inputs(seed: int = 0) -> dict:
    arg_keys = jax.random.split(jax.random.key(seed), 11)
    return {
        "queries": draw_queries(jax.random.fold_in(arg_keys[10], 71), 0),
        "keys": draw_keys(jax.random.fold_in(arg_keys[10], 71), 0),
        "values": gaussian(arg_keys[2], (TOKENS, KV_HEADS * HEAD_DIM), 1.0, 6.0, ((0, 16), (1, 8))),
        "dt_logits": draw_dt_logits(jax.random.fold_in(arg_keys[10], 71), 0),
        "decay_log": draw_decay_log(jax.random.fold_in(arg_keys[10], 71), 0),
        "dt_bias": jnp.clip(jax.random.uniform(arg_keys[5], (HEADS,), jnp.float32, -1.0, 1.0) * block_levels(arg_keys[5], (HEADS,), ((0, 8),), -0.4, 0.0), -1.0, 1.0),
        "c_weight": gaussian(arg_keys[6], (HEADS, HEAD_DIM, STATE), HEAD_DIM ** -0.5, 0.5, ((0, 8),)),
        "b_weight": gaussian(arg_keys[7], (HEADS, HEAD_DIM, STATE), HEAD_DIM ** -0.5, 0.5, ((0, 8),)),
        "x_weight": gaussian(arg_keys[8], (HEADS, HEAD_DIM, HEAD_DIM), HEAD_DIM ** -0.5, 0.5, ((0, 8),)),
        "norm_gain": jnp.clip(1.0 + 0.1 * jax.random.normal(arg_keys[9], (HEADS * HEAD_DIM,), jnp.float32), 0.5, 1.5),
    }


epsilon = 1e-05
highest = lax.Precision.HIGHEST

def by_position(stacked):
    layout = stacked.shape
    return stacked.reshape((STRIDE, TOK_DEV) + layout[1:]).swapaxes(0, 1).reshape(layout)

def project(q_feats, k_feats, v_feats, dt_raw, c_map, b_map, x_map, decay_log, dt_bias):
    head_count = c_map.shape[0]
    kv_count = k_feats.shape[1]
    group_size = head_count // kv_count
    head_dim = c_map.shape[1]
    state_dim = c_map.shape[2]
    row_count = q_feats.shape[0]
    c_mat = jnp.einsum('rhd,hdn->rhn', q_feats, c_map, precision=highest) * state_dim ** (-0.5)
    b_mat = jnp.einsum('rkd,kgdn->rkgn', k_feats, b_map.reshape(kv_count, group_size, head_dim, state_dim), precision=highest)
    x_mat = jnp.einsum('rkd,kgdp->rkgp', v_feats, x_map.reshape(kv_count, group_size, head_dim, head_dim), precision=highest)
    b_mat = b_mat.reshape(row_count, head_count, state_dim)
    x_mat = x_mat.reshape(row_count, head_count, head_dim)
    dt_step = jax.nn.softplus(dt_raw + dt_bias)
    log_keep = -jnp.exp(decay_log) * dt_step
    return (c_mat, b_mat, x_mat, dt_step, log_keep)

def run_stretches(c_mat, b_mat, x_mat, dt_step, log_keep, state, stretch_len):
    row_count = c_mat.shape[0]
    stretch_count = row_count // stretch_len

    def split_rows(matrix):
        return matrix.reshape((stretch_count, stretch_len) + matrix.shape[1:])
    causal = jnp.arange(stretch_len)[:, None] >= jnp.arange(stretch_len)[None, :]

    def advance(carried, pieces):
        c_blk, b_blk, x_blk, dt_blk, keep_blk = pieces
        running = jnp.cumsum(keep_blk, axis=0)
        spans = running.T[:, :, None] - running.T[:, None, :]
        decay = jnp.where(causal, jnp.exp(jnp.where(causal, spans, 0.0)), 0.0) * dt_blk.T[:, None, :]
        scores = jnp.einsum('ihn,jhn->hij', c_blk, b_blk, precision=highest)
        inside = jnp.einsum('hij,jhp->ihp', scores * decay, x_blk, precision=highest)
        carried_in = jnp.einsum('ihn,hnp->ihp', c_blk * jnp.exp(running)[:, :, None], carried, precision=highest)
        ending = running[-1]
        weights = jnp.exp(ending[None, :] - running) * dt_blk
        fresh = jnp.einsum('jhn,jhp->hnp', b_blk * weights[:, :, None], x_blk, precision=highest)
        return (jnp.exp(ending)[:, None, None] * carried + fresh, inside + carried_in)
    final_state, outputs = lax.scan(advance, state, (split_rows(c_mat), split_rows(b_mat), split_rows(x_mat), split_rows(dt_step), split_rows(log_keep)))
    return (outputs.reshape((row_count,) + outputs.shape[2:]), final_state)

def teacher(q_pos, k_pos, v_pos):
    group_size = HEADS // KV_HEADS
    q_all = q_pos.astype(jnp.float32).reshape(TOKENS, KV_HEADS, group_size, HEAD_DIM).transpose(1, 0, 2, 3)
    k_all = k_pos.astype(jnp.float32).reshape(TOKENS, KV_HEADS, HEAD_DIM).transpose(1, 0, 2)
    v_all = v_pos.astype(jnp.float32).reshape(TOKENS, KV_HEADS, HEAD_DIM).transpose(1, 0, 2)
    pieces = []
    for block_number in range(STRIDE):
        low = block_number * TOK_DEV
        high = low + TOK_DEV
        visible = jnp.arange(high)[None, :] <= jnp.arange(low, high)[:, None]

        def one_head(member, visible=visible):
            q_head, k_head, v_head = member
            scores = jnp.einsum('lgd,md->glm', q_head, k_head, precision=highest) * HEAD_DIM ** (-0.5)
            scores = jnp.where(visible[None], scores, -jnp.inf)
            highest_score = lax.optimization_barrier(jnp.max(scores, axis=2, keepdims=True))
            weights = jnp.exp(scores - highest_score)
            row_total = lax.optimization_barrier(jnp.sum(weights, axis=2))
            mixed = jnp.einsum('glm,md->lgd', weights, v_head, precision=highest)
            return mixed / row_total.T[:, :, None]
        block_out = lax.map(one_head, (q_all[:, low:high], k_all[:, :high], v_all[:, :high]))
        pieces.append(block_out.transpose(1, 0, 2, 3).reshape(TOK_DEV, HEADS * HEAD_DIM).astype(jnp.bfloat16))
    return jnp.concatenate(pieces, axis=0)

def reference(queries, keys, values, dt_logits, decay_log, dt_bias, c_weight, b_weight, x_weight, norm_gain):
    q_pos = by_position(queries)
    k_pos = by_position(keys)
    v_pos = by_position(values)
    z_pos = by_position(dt_logits)
    teacher_rows = teacher(q_pos, k_pos, v_pos).astype(jnp.float32)
    target = teacher_rows * lax.rsqrt(lax.optimization_barrier(jnp.mean(teacher_rows * teacher_rows, axis=1)) + epsilon)[:, None]
    q_feats = q_pos.astype(jnp.float32).reshape(TOKENS, HEADS, HEAD_DIM)
    k_feats = k_pos.astype(jnp.float32).reshape(TOKENS, KV_HEADS, HEAD_DIM)
    v_feats = v_pos.astype(jnp.float32).reshape(TOKENS, KV_HEADS, HEAD_DIM)
    z_feats = z_pos.astype(jnp.float32)

    def objective(c_map, b_map, x_map, log_rate, bias_vec, gain_vec):
        c_mat, b_mat, x_mat, dt_step, log_keep = project(q_feats, k_feats, v_feats, z_feats, c_map, b_map, x_map, log_rate, bias_vec)
        start_state = jnp.zeros((HEADS, STATE, HEAD_DIM), jnp.float32)
        mixed, unused_state = run_stretches(c_mat, b_mat, x_mat, dt_step, log_keep, start_state, STRETCH)
        flat = mixed.reshape(TOKENS, HEADS * HEAD_DIM)
        inverse = lax.rsqrt(lax.optimization_barrier(jnp.mean(flat * flat, axis=1)) + epsilon)
        normed = flat * inverse[:, None] * gain_vec
        loss = jnp.sum((normed - target) ** 2) / TOKENS
        return (loss, normed)
    loss, undo_loss, normed = jax.vjp(objective, c_weight.astype(jnp.float32), b_weight.astype(jnp.float32), x_weight.astype(jnp.float32), decay_log, dt_bias, norm_gain, has_aux=True)
    grad_c, grad_b, grad_x, grad_decay, grad_bias, grad_gain = undo_loss(jnp.ones_like(loss))
    return (normed.astype(jnp.bfloat16), grad_c, grad_b, grad_x, grad_decay, grad_bias, grad_gain)
```

```python
import jax
import jax.numpy as jnp
from jax import lax
from jax.experimental import pallas as pl
from jax.experimental.pallas import tpu as pltpu
from jax.sharding import PartitionSpec as P

MESH = pl.DeviceIdType.MESH
F32 = jnp.float32
BF16 = jnp.bfloat16
HEADS = 8
DIM = 128
ROWS = 256
CTX = 16
TP = 8
CHIPS = CTX // 2
SUB = ROWS // CTX
PIECES = 4
PIECE = ROWS // PIECES
BLOCKS = CTX // PIECES
TOKENS = ROWS * CTX
FEATURES = HEADS * DIM * TP
EPS = 1e-05
SCALE = DIM**-0.5
LOG2E = 1.4426950408889634
PAIR = 2
NEG = -1e30


def nn(a, b):
    return lax.dot_general(a, b, (((1,), (0,)), ((), ())), preferred_element_type=F32)


def nt(a, b):
    return lax.dot_general(a, b, (((1,), (1,)), ((), ())), preferred_element_type=F32)


def split(value):
    high = value.astype(BF16)
    return high, (value - high.astype(F32)).astype(BF16)


def wide(value):
    return jnp.concatenate(split(value), axis=1)


def twice(value, axis):
    return jnp.concatenate([value, value], axis=axis)


def halves(value):
    return value[:, :DIM] + value[:, DIM:]


def by_mask(value, mask):
    first = value.astype(BF16)
    rest = value - first.astype(F32)
    second = rest.astype(BF16)
    third = (rest - second.astype(F32)).astype(BF16)
    return nn(first, mask) + nn(second, mask) + nn(third, mask)


def product(a, b):
    a_high, a_low = split(a)
    b_high, b_low = split(b)
    return halves(nn(a_high, jnp.concatenate([b_high, b_low], axis=1))) + nn(a_low, b_high)


def product_t(a, b):
    a_high, a_low = split(a)
    b_high, b_low = split(b)
    return nt(jnp.concatenate([a_high, a_low], axis=1), twice(b_high, 1)) + nt(a_high, b_low)


def iota(shape, axis):
    return lax.broadcasted_iota(jnp.int32, shape, axis)


def place(row):
    return (row & 15) * 16 + (row >> 4)


def columns_of(rows):
    return jnp.concatenate([rows, jnp.zeros((DIM - 8, ROWS), F32)], axis=0).T


def steps_of(logits, bias):
    raised = logits + bias
    faded = jnp.exp(-jnp.abs(raised))
    step = jnp.maximum(raised, 0.0) + jnp.log1p(faded)
    slope = jnp.where(raised >= 0.0, 1.0, faded) / (1.0 + faded)
    return step, slope


def kernel(
    q_in, k_in, v_in, z_in, decay_in, bias_in, c_w, b_w, x_w, gain_in,
    out, grad_c, grad_b, grad_x, grad_small,
    qr, kv, zall, kpos, vpos, qh, acc, top, tq, mom, wts, rows, rcol, rbcol, kown, vown,
    t_all, s_all, d_all, z_all, y_all, stats, stx, cols, decay_part, bias_part,
    gbuf, sibr, pairsum, rs, fin, small,
    local_sem, q_ss, q_rs, z_ss, z_rs, kv_ss, kv_rs, t_ss, t_rs, sib_ss, sib_rs, r_ss, r_rs,
    ag_ss, ag_rs, fw_ss, fw_rs, sm_ss, sm_rs,
):
    me = lax.axis_index("ctx")
    tp = lax.axis_index("tp")
    core = lax.rem(me, 2)
    chip = me // 2
    sibling = me + 1 - 2 * core

    def remote(src, dst, send, recv, where):
        return pltpu.make_async_remote_copy(
            src_ref=src, dst_ref=dst, send_sem=send, recv_sem=recv, device_id=where, device_id_type=MESH
        )

    def others(count, mine, body):
        def one(step, carry):
            body(lax.rem(mine + step, count))
            return carry

        lax.fori_loop(1, count, one, 0)

    def each(count, body):
        def one(step, carry):
            body(step)
            return carry

        lax.fori_loop(0, count, one, 0)

    def clear(source):
        kv[source] = jnp.zeros((ROWS, 2 * DIM), BF16)

    each(CTX, clear)
    own_rows = pl.ds(pl.multiple_of(SUB * me, SUB), SUB)
    own = [
        pltpu.make_async_copy(k_in, kv.at[me, :, pl.ds(0, DIM)], local_sem.at[0]),
        pltpu.make_async_copy(v_in, kv.at[me, :, pl.ds(DIM, DIM)], local_sem.at[1]),
        pltpu.make_async_copy(q_in.at[own_rows], qr.at[me], local_sem.at[2]),
    ]
    for copy in own:
        copy.start()
    zall[me] = z_in[...]
    barrier = pltpu.get_barrier_semaphore()
    others(CTX, me, lambda peer: pl.semaphore_signal(barrier, inc=1, device_id={"ctx": peer}, device_id_type=MESH))
    others(TP, tp, lambda peer: pl.semaphore_signal(barrier, inc=1, device_id={"tp": peer}, device_id_type=MESH))
    for copy in own:
        copy.wait()
    pl.semaphore_wait(barrier, CTX - 1 + TP - 1)

    def q_copy(peer, slot):
        taken = pl.ds(pl.multiple_of(SUB * peer, SUB), SUB)
        return remote(q_in.at[taken], qr.at[slot], q_ss.at[peer], q_rs.at[slot], {"ctx": peer})

    def z_copy(peer, slot):
        return remote(zall.at[slot], zall.at[slot], z_ss.at[peer], z_rs.at[slot], {"ctx": peer})

    def kv_copy(peer, slot, piece):
        part = pl.ds(pl.multiple_of(PIECE * piece, PIECE), PIECE)
        return remote(
            kv.at[slot, part], kv.at[slot, part], kv_ss.at[peer, piece], kv_rs.at[slot, piece], {"ctx": peer}
        )

    others(CTX, me, lambda peer: z_copy(peer, me).start())
    others(CTX, me, lambda peer: q_copy(peer, me).start())

    def send_piece(piece):
        def send(peer):
            @pl.when(peer >= BLOCKS * piece)
            def _():
                kv_copy(peer, me, piece).start()

        others(CTX, me, send)

    each(PIECES, send_piece)

    others(CTX, me, lambda peer: z_copy(peer, peer).wait_recv())
    logits = zall[...]
    speed = -jnp.exp(decay_in[...])
    step, slope = steps_of(logits, bias_in[...][None])
    rate = speed[None] * step
    rate_b = speed[None] * slope
    lower = iota((ROWS, ROWS), 0)
    upper = iota((ROWS, ROWS), 1)
    after = jnp.where((lower > upper) & (lower < SUB * me), 1.0, 0.0).astype(BF16)
    span = by_mask(jnp.sum(rate, axis=0), after)
    span_b = by_mask(jnp.sum(rate_b, axis=0), after)
    earlier = iota((HEADS, ROWS), 1) < SUB * me
    for source in reversed(range(CTX)):
        weight = jnp.where(earlier, jnp.exp(span) * step[source], 0.0)
        wts[0, source] = weight
        wts[1, source] = weight * span
        wts[2, source] = weight * (span_b + slope[source] / step[source])
        span = span + rate[source]
        span_b = span_b + rate_b[source]

    pick = jnp.where(lower == SUB * me + (upper & 15), 1.0, 0.0).astype(BF16)
    picked = nn(logits.reshape(CTX * HEADS, ROWS).astype(BF16), pick).reshape(CTX, HEADS, ROWS)
    matched = iota((CTX, HEADS, ROWS), 0) == (iota((CTX, HEADS, ROWS), 2) >> 4)
    own_logits = jnp.sum(jnp.where(matched, picked, 0.0), axis=0)
    own_step, own_slope = steps_of(own_logits, bias_in[...])
    until = jnp.where(place(lower) <= place(upper), 1.0, 0.0).astype(BF16)
    running = by_mask(speed * own_step, until)
    running_b = by_mask(speed * own_slope, until)
    rows[0] = running
    rows[1] = own_step
    rows[2] = running_b
    rows[3] = own_slope / own_step
    running_c = columns_of(running)
    running_bc = columns_of(running_b)
    for head in range(HEADS):
        rcol[head] = jnp.broadcast_to(running_c[:, head : head + 1], (ROWS, DIM))
        rbcol[head] = jnp.broadcast_to(running_bc[:, head : head + 1], (ROWS, DIM))

    others(CTX, me, lambda peer: q_copy(peer, peer).wait_recv())
    for head in range(HEADS):
        qh[head] = qr[:, :, head * DIM : (head + 1) * DIM].reshape(ROWS, DIM)
        acc[head] = jnp.zeros((ROWS, 2 * DIM), F32)
        top[head] = jnp.full((ROWS, DIM), NEG, F32)

    def attend(chunk, group, masked):
        heads = pl.ds(PAIR * group, PAIR)
        query = qh[heads].reshape(PAIR * ROWS, DIM)
        key = kpos[pl.ds(2 * chunk, 2)].reshape(2 * ROWS, DIM)
        value = vpos[pl.ds(2 * chunk, 2)].reshape(2 * ROWS, 2 * DIM)
        scores = nt(query, key) * (SCALE * LOG2E)
        if masked:
            at_q = place(iota(scores.shape, 0) & (ROWS - 1)) + ROWS * me
            lane = iota(scores.shape, 1)
            at_k = place(lane & (ROWS - 1)) + (lane >> 8) * ROWS + 2 * ROWS * chunk
            scores = jnp.where(at_k <= at_q, scores, NEG)
        old = top[heads].reshape(PAIR * ROWS, DIM)
        new = jnp.maximum(old, jnp.max(scores, axis=1, keepdims=True))
        weights = jnp.exp2(scores - new[:, :1])
        shrink = jnp.exp2(old - new)
        mixed = nn(weights.astype(BF16), value)
        total = acc[heads].reshape(PAIR * ROWS, 2 * DIM)
        acc[heads] = (total * twice(shrink, 1) + mixed).reshape(PAIR, ROWS, 2 * DIM)
        top[heads] = new.reshape(PAIR, ROWS, DIM)

    def fold_piece(piece):
        def arrived(peer):
            kv_copy(peer, peer, piece).wait_recv()

        others(CTX, me, arrived)

        def sort(index):
            block = BLOCKS * piece + index
            part = pl.ds(pl.multiple_of(SUB * block, SUB), SUB)
            both = kv[:, part, :].reshape(ROWS, 2 * DIM)
            kpos[block] = both[:, :DIM]
            vpos[block, :, :DIM] = both[:, DIM:]
            vpos[block, :, DIM:] = jnp.ones((ROWS, DIM), BF16)

        each(BLOCKS, sort)

        def over(chunk, carry):
            each(HEADS // PAIR, lambda group: attend(chunk, group, False))
            return carry

        first = piece * (BLOCKS // 2)
        lax.fori_loop(first, jnp.minimum(first + BLOCKS // 2, chip), over, 0)

    each(me // BLOCKS + 1, fold_piece)
    each(HEADS // PAIR, lambda group: attend(chip, group, True))

    def close(head):
        total = acc[head]
        tq[head] = (total[:, :DIM] / total[:, DIM:]).astype(BF16)

    each(HEADS, close)

    mom[...] = jnp.zeros_like(mom)

    def moments(source):
        both = kv[source]
        key_t = both[:, :DIM].astype(F32).T
        value = both[:, DIM:]
        for head in range(HEADS):
            high, low = split(key_t * wts[0, source, head : head + 1, :])
            by_decay = (key_t * wts[1, source, head : head + 1, :]).astype(BF16)
            by_bias = (key_t * wts[2, source, head : head + 1, :]).astype(BF16)
            stacked = jnp.concatenate([high, low, by_decay, by_bias], axis=0)
            mom[head] = mom[head] + nn(stacked, value)

    each(CTX, moments)

    own_kv = kv[:, own_rows, :].reshape(ROWS, 2 * DIM)
    kown[...] = twice(own_kv[:, :DIM], 1)
    vown[...] = twice(own_kv[:, DIM:], 1)
    stats[...] = jnp.zeros_like(stats)

    def decays(head):
        causal = place(iota((ROWS, ROWS), 1)) <= place(iota((ROWS, ROWS), 0))
        gap = twice(rcol[head], 1) - rows[0, pl.ds(head, 1), :]
        return jnp.where(causal, jnp.exp(gap), 0.0) * rows[1, pl.ds(head, 1), :]

    def forward(head):
        mapped = wide(nt(c_w[head], b_w[head]) * SCALE)
        read = halves(nn(qh[head], mapped))
        t_all[head] = read
        score = nt(wide(read), kown[...])
        s_all[head] = score
        decay = decays(head)
        d_all[head] = decay
        high, low = split(score * decay)
        value = vown[:, :DIM]
        state = mom[head, 0:DIM] + mom[head, DIM : 2 * DIM]
        mixed = nn(high, value) + nn(low, value) + jnp.exp(rcol[head]) * product(read, state)
        z_all[head] = mixed
        flat = nn(wide(mixed), twice(x_w[head], 0))
        y_all[head] = flat
        taught = tq[head].astype(F32)
        scaled = flat * gain_in[pl.ds(head, 1), :]
        stats[0] += flat * flat
        stats[1] += taught * taught
        stats[2] += scaled * scaled
        stats[3] += scaled * taught

    each(HEADS, forward)

    lane = iota((ROWS, DIM), 1)
    packed = jnp.zeros((ROWS, DIM), F32)
    for index in range(4):
        packed = jnp.where(lane == index, jnp.sum(stats[index], axis=1, keepdims=True), packed)
    stx[tp] = packed.T[:8]

    def t_copy(peer, slot):
        return remote(stx.at[slot], stx.at[slot], t_ss.at[peer], t_rs.at[slot], {"tp": peer})

    others(TP, tp, lambda peer: t_copy(peer, tp).start())
    others(TP, tp, lambda peer: t_copy(peer, peer).wait_recv())
    sums = jnp.sum(stx[...], axis=0)
    inverse = lax.rsqrt(sums[0:1] / FEATURES + EPS)
    inverse_t = lax.rsqrt(sums[1:2] / FEATURES + EPS)
    cross = (2.0 / TOKENS) * (inverse * sums[2:3] - inverse_t * sums[3:4])
    pull = inverse * inverse * inverse * cross / FEATURES
    line = iota((8, ROWS), 0)
    spread = columns_of(jnp.where(line == 0, inverse, jnp.where(line == 1, inverse_t, pull)))
    for index in range(3):
        cols[index] = jnp.broadcast_to(spread[:, index : index + 1], (ROWS, DIM))

    order = jnp.where(iota((ROWS, ROWS), 0) == place(iota((ROWS, ROWS), 1)), 1.0, 0.0).astype(BF16)

    def sib_copy(head):
        return remote(gbuf.at[1 - core, head], sibr.at[head], sib_ss.at[head], sib_rs.at[head], {"ctx": sibling})

    def r_copy(head, slot):
        return remote(pairsum.at[head], rs.at[slot], r_ss.at[head], r_rs.at[slot], {"ctx": 2 * head + core})

    def pass_on(head):
        sib_copy(head).wait_recv()
        pairsum[head] = gbuf[core, head] + sibr[head]

        @pl.when(head != chip)
        def _():
            r_copy(head, chip).start()

        @pl.when(head == chip)
        def _():
            rs[chip] = pairsum[head]

    def backward(head):
        flat = y_all[head]
        gain = gain_in[pl.ds(head, 1), :]
        inv = cols[0]
        unit = flat * inv
        normed = unit * gain
        out[:, pl.ds(pl.multiple_of(head * DIM, DIM), DIM)] = nn(order, normed.astype(BF16)).astype(BF16)
        d_normed = (2.0 / TOKENS) * (normed - tq[head].astype(F32) * cols[1])
        small[me, pl.ds(head, 1), :] = jnp.sum(d_normed * unit, axis=0, keepdims=True)
        d_flat = d_normed * gain * inv - flat * cols[2]
        moved = d_flat * flat
        run = rcol[head]
        by_decay = jnp.sum(moved * run, axis=0, keepdims=True)
        by_bias = jnp.sum(moved * rbcol[head], axis=0, keepdims=True)
        mixed = z_all[head]
        gbuf[1, head] = product(mixed.T, d_flat)
        d_mixed = nt(wide(d_flat), twice(x_w[head], 1))
        d_score = nt(wide(d_mixed), vown[...]) * d_all[head]
        felt = jnp.sum(d_score * s_all[head], axis=0, keepdims=True)
        from_decay = felt * rows[0, pl.ds(head, 1), :]
        from_bias = felt * (rows[3, pl.ds(head, 1), :] - rows[2, pl.ds(head, 1), :])
        by_decay = by_decay - halves(from_decay)
        by_bias = by_bias + halves(from_bias)
        high, low = split(d_score)
        key = kown[:, :DIM]
        d_late = jnp.exp(run) * d_mixed
        state = mom[head, 0:DIM] + mom[head, DIM : 2 * DIM]
        d_read = nn(high, key) + nn(low, key) + product_t(d_late, state)
        d_state = product(t_all[head].T, d_late)
        by_decay = by_decay + jnp.sum(d_state * mom[head, 2 * DIM : 3 * DIM], axis=0, keepdims=True)
        by_bias = by_bias + jnp.sum(d_state * mom[head, 3 * DIM : 4 * DIM], axis=0, keepdims=True)
        decay_part[pl.ds(head, 1), :] = by_decay
        bias_part[pl.ds(head, 1), :] = by_bias
        query_t = qh[head].astype(F32).T.astype(BF16)
        gbuf[0, head] = halves(nn(query_t, wide(d_read)))
        sib_copy(head).start()

        @pl.when(head > 0)
        def _():
            pass_on(head - 1)

    each(HEADS, backward)
    pass_on(HEADS - 1)
    line = iota((HEADS, DIM), 1)
    decay_sum = jnp.sum(decay_part[...], axis=1, keepdims=True)
    bias_sum = jnp.sum(bias_part[...], axis=1, keepdims=True)
    small[me, HEADS:, :] = jnp.where(line == 0, decay_sum, jnp.where(line == 1, bias_sum, 0.0))

    def sm_copy(peer, slot):
        return remote(small.at[slot], small.at[slot], sm_ss.at[peer], sm_rs.at[slot], {"ctx": peer})

    others(CTX, me, lambda peer: sm_copy(peer, me).start())

    others(CHIPS, chip, lambda peer: r_copy(peer, peer).wait_recv())
    fin[core, chip] = jnp.sum(rs[...], axis=0)

    def ag_copy(peer, slot):
        held = fin.at[core, slot]
        return remote(held, held, ag_ss.at[peer], ag_rs.at[slot], {"ctx": 2 * peer + core})

    def fw_copy(slot, side):
        held = fin.at[side, slot]
        return remote(held, held, fw_ss.at[slot], fw_rs.at[slot], {"ctx": sibling})

    others(CHIPS, chip, lambda peer: ag_copy(peer, chip).start())
    fw_copy(chip, core).start()

    def hand_over(peer):
        ag_copy(peer, peer).wait_recv()
        fw_copy(peer, core).start()

    others(CHIPS, chip, hand_over)

    def finish(head):
        fw_copy(head, 1 - core).wait_recv()
        grad_x[head] = fin[1, head]
        joint = fin[0, head]
        grad_c[head] = nn(wide(joint), twice(b_w[head], 0)) * SCALE
        grad_b[head] = nn(wide(joint.T), twice(c_w[head], 0)) * SCALE

    each(HEADS, finish)
    others(CTX, me, lambda peer: sm_copy(peer, peer).wait_recv())
    grad_small[...] = jnp.sum(small[...], axis=0)

    def left(peer):
        z_copy(peer, me).wait_send()
        q_copy(peer, me).wait_send()
        sm_copy(peer, me).wait_send()

    others(CTX, me, left)

    def left_piece(piece):
        def one(peer):
            @pl.when(peer >= BLOCKS * piece)
            def _():
                kv_copy(peer, me, piece).wait_send()

        others(CTX, me, one)

    each(PIECES, left_piece)
    others(TP, tp, lambda peer: t_copy(peer, tp).wait_send())
    others(CHIPS, chip, lambda peer: r_copy(peer, chip).wait_send())
    others(CHIPS, chip, lambda peer: ag_copy(peer, chip).wait_send())

    def left_pair(head):
        sib_copy(head).wait_send()
        fw_copy(head, core).wait_send()

    each(HEADS, left_pair)


def local(queries, keys, values, dt_logits, decay_log, dt_bias, c_weight, b_weight, x_weight, norm_gain):
    whole = pl.BlockSpec(memory_space=pltpu.VMEM)
    there = pl.BlockSpec(memory_space=pl.ANY)
    dma = pltpu.SemaphoreType.DMA

    def f32(*shape):
        return pltpu.VMEM(shape, F32)

    def bf16(*shape):
        return pltpu.VMEM(shape, BF16)

    square = (HEADS, DIM, DIM)
    by_row = (HEADS, ROWS, DIM)
    out, grad_c, grad_b, grad_x, small = pl.pallas_call(
        kernel,
        out_shape=(
            jax.ShapeDtypeStruct((ROWS, HEADS * DIM), BF16),
            jax.ShapeDtypeStruct(square, F32),
            jax.ShapeDtypeStruct(square, F32),
            jax.ShapeDtypeStruct(square, F32),
            jax.ShapeDtypeStruct((2 * HEADS, DIM), F32),
        ),
        in_specs=[there] * 3 + [whole] * 7,
        out_specs=[whole] * 5,
        scratch_shapes=[
            bf16(CTX, SUB, HEADS * DIM),
            bf16(CTX, ROWS, 2 * DIM),
            f32(CTX, HEADS, ROWS),
            bf16(CTX, ROWS, DIM),
            bf16(CTX, ROWS, 2 * DIM),
            bf16(*by_row),
            f32(HEADS, ROWS, 2 * DIM),
            f32(*by_row),
            bf16(*by_row),
            f32(HEADS, 4 * DIM, DIM),
            f32(3, CTX, HEADS, ROWS),
            f32(4, HEADS, ROWS),
            f32(*by_row),
            f32(*by_row),
            bf16(ROWS, 2 * DIM),
            bf16(ROWS, 2 * DIM),
            f32(*by_row),
            f32(HEADS, ROWS, ROWS),
            f32(HEADS, ROWS, ROWS),
            f32(*by_row),
            f32(*by_row),
            f32(4, ROWS, DIM),
            f32(TP, 8, ROWS),
            f32(3, ROWS, DIM),
            f32(HEADS, DIM),
            f32(HEADS, DIM),
            f32(2, *square),
            f32(*square),
            f32(*square),
            f32(CHIPS, DIM, DIM),
            f32(2, *square),
            f32(CTX, 2 * HEADS, DIM),
            dma((3,)),
            dma((CTX,)), dma((CTX,)), dma((CTX,)), dma((CTX,)),
            dma((CTX, PIECES)), dma((CTX, PIECES)),
            dma((TP,)), dma((TP,)),
            dma((HEADS,)), dma((HEADS,)), dma((CHIPS,)), dma((CHIPS,)),
            dma((CHIPS,)), dma((CHIPS,)), dma((HEADS,)), dma((HEADS,)),
            dma((CTX,)), dma((CTX,)),
        ],
        compiler_params=pltpu.CompilerParams(
            collective_id=0, has_side_effects=True, vmem_limit_bytes=56 * 2**20
        ),
    )(
        queries, keys, values, dt_logits.astype(F32).T, decay_log.reshape(HEADS, 1), dt_bias.reshape(HEADS, 1),
        c_weight, b_weight, x_weight, norm_gain.reshape(HEADS, DIM),
    )
    return out, grad_c, grad_b, grad_x, small[HEADS:, 0], small[HEADS:, 1], small[:HEADS].reshape(-1)


def solution(mesh):
    return jax.shard_map(
        local,
        mesh=mesh,
        in_specs=(
            P("ctx", "tp"),
            P("ctx", "tp"),
            P("ctx", "tp"),
            P("ctx", "tp"),
            P("tp"),
            P("tp"),
            P("tp", None, None),
            P("tp", None, None),
            P("tp", None, None),
            P("tp"),
        ),
        out_specs=(
            P("ctx", "tp"),
            P("tp", None, None),
            P("tp", None, None),
            P("tp", None, None),
            P("tp"),
            P("tp"),
            P("tp"),
        ),
        check_vma=False,
    )
```

```python
import jax
import jax.numpy as jnp
from jax import lax
from jax.experimental import pallas as pl
from jax.experimental.pallas import tpu as pltpu
from jax.sharding import PartitionSpec as P

MESH = pl.DeviceIdType.MESH
F32 = jnp.float32
BF16 = jnp.bfloat16
HEADS = 8
DIM = 128
ROWS = 256
CTX = 16
TP = 8
CHIPS = CTX // 2
SUB = ROWS // CTX
PIECES = 2
PIECE = ROWS // PIECES
WIDTH = 4
STEPS = CTX // PIECES // WIDTH
QUAD = 4
HEAD_ROWS = 16
TAIL = 8
GROUP = 2
TOKENS = ROWS * CTX
FEATURES = HEADS * DIM * TP
EPS = 1e-05
SCALE = DIM**-0.5
LOG2E = 1.4426950408889634
NEG = -1e30


def nn(a, b):
    return lax.dot_general(a, b, (((1,), (0,)), ((), ())), preferred_element_type=F32)


def nt(a, b):
    return lax.dot_general(a, b, (((1,), (1,)), ((), ())), preferred_element_type=F32)


def split(value):
    high = value.astype(BF16)
    return high, (value - high.astype(F32)).astype(BF16)


def wide(value):
    return jnp.concatenate(split(value), axis=1)


def twice(value, axis):
    return jnp.concatenate([value, value], axis=axis)


def halves(value):
    return value[:, :DIM] + value[:, DIM:]


def by_mask(value, mask):
    first = value.astype(BF16)
    rest = value - first.astype(F32)
    second = rest.astype(BF16)
    third = (rest - second.astype(F32)).astype(BF16)
    return nn(first, mask) + nn(second, mask) + nn(third, mask)


def product(a, b):
    a_high, a_low = split(a)
    b_high, b_low = split(b)
    return halves(nn(a_high, jnp.concatenate([b_high, b_low], axis=1))) + nn(a_low, b_high)


def product_t(a, b):
    a_high, a_low = split(a)
    b_high, b_low = split(b)
    return nt(jnp.concatenate([a_high, a_low], axis=1), twice(b_high, 1)) + nt(a_high, b_low)


def iota(shape, axis):
    return lax.broadcasted_iota(jnp.int32, shape, axis)


def place(row):
    return (row & 15) * 16 + (row >> 4)


def columns_of(rows):
    return jnp.concatenate([rows, jnp.zeros((DIM - 8, ROWS), F32)], axis=0).T


def steps_of(logits, bias):
    raised = logits + bias
    faded = jnp.exp(-jnp.abs(raised))
    step = jnp.maximum(raised, 0.0) + jnp.log1p(faded)
    slope = jnp.where(raised >= 0.0, 1.0, faded) / (1.0 + faded)
    return step, slope


def kernel(
    q_in, k_in, v_in, z_in, decay_in, bias_in, c_in, b_in, x_in, gain_in,
    out_to, fin_to,
    qr, kv, kpos, vpos, qh, hide, acc, top, tq, mom, tangent, wts, rows, rcol, rbcol, kown, vown, gains,
    c_w, b_w, x_w, t_all, s_all, d_all, z_all, y_all, stats, stx, cols, out,
    gbuf, sibr, pairsum, rs, fin,
    local_sem, w_sem, out_sem, q_ss, q_rs, kv_ss, kv_rs, kf_ss, kf_rs, t_ss, t_rs, sib_ss, sib_rs, r_ss, r_rs,
    ag_ss, ag_rs, fw_ss, fw_rs,
):
    me = lax.axis_index("ctx")
    tp = lax.axis_index("tp")
    core = lax.rem(me, 2)
    chip = me // 2
    sibling = me + 1 - 2 * core

    def remote(src, dst, send, recv, where):
        return pltpu.make_async_remote_copy(
            src_ref=src, dst_ref=dst, send_sem=send, recv_sem=recv, device_id=where, device_id_type=MESH
        )

    def others(count, mine, body):
        for step in range(1, count):
            body((mine + step) & (count - 1))

    def each(count, body):
        def one(step, carry):
            body(step)
            return carry

        lax.fori_loop(0, count, one, 0)

    own_rows = pl.ds(pl.multiple_of(SUB * me, SUB), SUB)
    body_rows = pl.ds(HEAD_ROWS, ROWS)
    own = [
        pltpu.make_async_copy(k_in, kv.at[me, body_rows, pl.ds(0, DIM)], local_sem.at[0]),
        pltpu.make_async_copy(v_in, kv.at[me, body_rows, pl.ds(DIM, DIM)], local_sem.at[1]),
        pltpu.make_async_copy(q_in.at[own_rows], qr.at[me], local_sem.at[2]),
    ]
    for copy in own:
        copy.start()
    weights = [
        pltpu.make_async_copy(c_in, c_w, w_sem.at[0]),
        pltpu.make_async_copy(b_in, b_w, w_sem.at[1]),
        pltpu.make_async_copy(x_in, x_w, w_sem.at[2]),
    ]
    for copy in weights:
        copy.start()
    barrier = pltpu.get_barrier_semaphore()
    others(CTX, me, lambda peer: pl.semaphore_signal(barrier, inc=1, device_id={"ctx": peer}, device_id_type=MESH))
    others(TP, tp, lambda peer: pl.semaphore_signal(barrier, inc=1, device_id={"tp": peer}, device_id_type=MESH))
    turn = jnp.where(iota((HEAD_ROWS, HEADS), 0) == iota((HEAD_ROWS, HEADS), 1), 1.0, 0.0).astype(BF16)
    kv[me, :HEAD_ROWS, :] = nt(turn, z_in[...]).astype(BF16)
    for copy in own:
        copy.wait()
    pl.semaphore_wait(barrier, CTX - 1 + TP - 1)

    def part_of(piece):
        if piece == 0:
            return pl.ds(0, HEAD_ROWS + PIECE)
        return pl.ds(HEAD_ROWS + PIECE * piece, PIECE)

    def kv_copy(peer, slot, piece):
        held = kv.at[2 * slot + core, part_of(piece)]
        return remote(held, held, kv_ss.at[peer, piece], kv_rs.at[slot, piece], {"ctx": 2 * peer + core})

    def kf_copy(slot, side, piece):
        held = kv.at[2 * slot + side, part_of(piece)]
        return remote(held, held, kf_ss.at[slot, piece], kf_rs.at[slot, piece], {"ctx": sibling})

    def needs(peer, piece):
        return peer >= piece * (CHIPS // PIECES)

    def q_copy(peer, slot):
        taken = pl.ds(pl.multiple_of(SUB * peer, SUB), SUB)
        return remote(q_in.at[taken], qr.at[slot], q_ss.at[peer], q_rs.at[slot], {"ctx": peer})

    def send_piece(piece):
        def send(peer):
            @pl.when(needs(peer, piece))
            def _():
                kv_copy(peer, chip, piece).start()

        others(CHIPS, chip, send)

        @pl.when(needs(chip, piece))
        def _():
            kf_copy(chip, core, piece).start()

    def relay(piece):
        def one(peer):
            kv_copy(peer, peer, piece).wait_recv()
            kf_copy(peer, core, piece).start()

        others(CHIPS, chip, one)

    def arrived(piece):
        kf_copy(chip, 1 - core, piece).wait_recv()
        others(CHIPS, chip, lambda peer: kf_copy(peer, 1 - core, piece).wait_recv())

    send_piece(0)
    others(CTX, me, lambda peer: q_copy(peer, me).start())
    for piece in range(1, PIECES):
        send_piece(piece)

    for head in range(HEADS):
        gains[head : head + 1, :] = gain_in[head * DIM : (head + 1) * DIM].reshape(1, DIM)
        acc[head] = jnp.zeros((ROWS, 2 * DIM), F32)
        top[head] = jnp.full((ROWS, DIM), NEG, F32)
    mom[...] = jnp.zeros_like(mom)
    tangent[...] = jnp.zeros_like(tangent)
    stats[...] = jnp.zeros_like(stats)
    last = me // WIDTH
    shown = (ROWS, WIDTH * ROWS)
    key_place = place(iota(shown, 1) & (ROWS - 1)) + (iota(shown, 1) >> 8) * ROWS + WIDTH * ROWS * last
    hide[...] = jnp.where(key_place <= place(iota(shown, 0)) + ROWS * me, 0.0, NEG)
    head_line = iota((HEADS, ROWS), 0)
    decay_rate = jnp.zeros((HEADS, ROWS), F32)
    bias = jnp.zeros((HEADS, ROWS), F32)
    for head in range(HEADS):
        decay_rate = jnp.where(head_line == head, decay_in[head], decay_rate)
        bias = jnp.where(head_line == head, bias_in[head], bias)
    speed = -jnp.exp(decay_rate)
    relay(0)
    arrived(0)

    logits = kv[:, :HEAD_ROWS, :].astype(F32)[:, :HEADS, :]
    step, slope = steps_of(logits, bias[None])
    rate = speed[None] * step
    rate_b = speed[None] * slope
    lower = iota((ROWS, ROWS), 0)
    upper = iota((ROWS, ROWS), 1)
    after = jnp.where((lower > upper) & (lower < SUB * me), 1.0, 0.0).astype(BF16)
    span = by_mask(jnp.sum(rate, axis=0), after)
    span_b = by_mask(jnp.sum(rate_b, axis=0), after)
    earlier = iota((HEADS, ROWS), 1) < SUB * me
    for source in reversed(range(CTX)):
        weight = jnp.where(earlier, jnp.exp(span) * step[source], 0.0)
        kinds = (weight, weight * span, weight * (span_b + slope[source] / step[source]))
        for index, kind in enumerate(kinds):
            for piece in range(PIECES):
                wts[index, piece, :, source * PIECE : (source + 1) * PIECE] = kind[:, piece * PIECE : (piece + 1) * PIECE]
        span = span + rate[source]
        span_b = span_b + rate_b[source]

    pick = jnp.where(lower == SUB * me + (upper & 15), 1.0, 0.0).astype(BF16)
    picked = nn(logits.reshape(CTX * HEADS, ROWS).astype(BF16), pick).reshape(CTX, HEADS, ROWS)
    matched = iota((CTX, HEADS, ROWS), 0) == (iota((CTX, HEADS, ROWS), 2) >> 4)
    own_logits = jnp.sum(jnp.where(matched, picked, 0.0), axis=0)
    own_step, own_slope = steps_of(own_logits, bias)
    until = jnp.where(place(lower) <= place(upper), 1.0, 0.0).astype(BF16)
    running = by_mask(speed * own_step, until)
    running_b = by_mask(speed * own_slope, until)
    rows[0] = running
    rows[1] = own_step
    rows[2] = running_b
    rows[3] = own_slope / own_step
    running_c = columns_of(running)
    running_bc = columns_of(running_b)
    for head in range(HEADS):
        rcol[head] = jnp.broadcast_to(running_c[:, head : head + 1], (ROWS, DIM))
        rbcol[head] = jnp.broadcast_to(running_bc[:, head : head + 1], (ROWS, DIM))

    def gathered(piece, quad):
        part = kv[pl.ds(QUAD * quad, QUAD), pl.ds(HEAD_ROWS + PIECE * piece, PIECE), :]
        both = part.reshape(QUAD * PIECE, 2 * DIM)
        lanes = pl.ds(pl.multiple_of(quad * QUAD * PIECE, QUAD * PIECE), QUAD * PIECE)
        return both[:, :DIM].astype(F32).T, both[:, DIM:], lanes

    def moments(piece):
        def one(quad):
            key_t, value, lanes = gathered(piece, quad)
            double = twice(value, 0)
            for head in range(HEADS):
                mom[head] += nn(wide(key_t * wts[0, piece, head : head + 1, lanes]), double)

        each(CTX // QUAD, one)

    def tangents(piece):
        def one(quad):
            key_t, value, lanes = gathered(piece, quad)
            for head in range(HEADS):
                by_decay = (key_t * wts[1, piece, head : head + 1, lanes]).astype(BF16)
                by_bias = (key_t * wts[2, piece, head : head + 1, lanes]).astype(BF16)
                tangent[head] += nn(jnp.concatenate([by_decay, by_bias], axis=0), value)

        each(CTX // QUAD, one)

    def sort(piece):
        def one(index):
            block = piece * (CTX // PIECES) + index
            part = pl.ds(pl.multiple_of(HEAD_ROWS + SUB * block, SUB), SUB)
            both = kv[:, part, :].reshape(ROWS, 2 * DIM)
            kpos[block] = both[:, :DIM]
            vpos[block, :, :DIM] = both[:, DIM:]
            vpos[block, :, DIM:] = jnp.ones((ROWS, DIM), BF16)

        each(CTX // PIECES, one)

    def attend(chunk, masked):
        blocks = pl.ds(WIDTH * chunk, WIDTH)
        key = kpos[blocks].reshape(WIDTH * ROWS, DIM)
        value = vpos[blocks].reshape(WIDTH * ROWS, 2 * DIM)

        def mix(head, weights, shrink):
            acc[head] = acc[head] * twice(shrink, 1) + nn(weights, value)

        scores = nt(qh[0], key)
        waiting = None
        for head in range(HEADS):
            following = nt(qh[head + 1], key) if head + 1 < HEADS else None
            if masked:
                scores = scores + hide[...]
            old = top[head]
            new = jnp.maximum(old, jnp.max(scores, axis=1, keepdims=True))
            weights = jnp.exp2((scores - new[:, :1]) * (SCALE * LOG2E)).astype(BF16)
            shrink = jnp.exp2((old - new) * (SCALE * LOG2E))
            top[head] = new
            if waiting is not None:
                mix(*waiting)
            waiting = (head, weights, shrink)
            scores = following
        mix(*waiting)

    def teach(piece):
        def over(chunk, carry):
            attend(chunk, False)
            return carry

        lax.fori_loop(STEPS * piece, jnp.minimum(STEPS * (piece + 1), last), over, 0)

    sort(0)
    moments(0)
    others(CTX, me, lambda peer: q_copy(peer, peer).wait_recv())
    for head in range(HEADS):
        qh[head] = qr[:, :, head * DIM : (head + 1) * DIM].reshape(ROWS, DIM)
    for piece in range(1, PIECES):

        @pl.when(needs(chip, piece))
        def _(piece=piece):
            relay(piece)

    teach(0)
    for piece in range(1, PIECES):

        @pl.when(needs(chip, piece))
        def _(piece=piece):
            arrived(piece)
            sort(piece)
            moments(piece)
            teach(piece)

    attend(last, True)

    def close(head):
        total = acc[head]
        tq[head] = (total[:, :DIM] / total[:, DIM:]).astype(BF16)

    each(HEADS, close)

    for copy in weights:
        copy.wait()
    own_kv = kv[:, pl.ds(pl.multiple_of(HEAD_ROWS + SUB * me, SUB), SUB), :].reshape(ROWS, 2 * DIM)
    kown[...] = twice(own_kv[:, :DIM], 1)
    vown[...] = twice(own_kv[:, DIM:], 1)

    def forward(group):
        heads = [GROUP * group + index for index in range(GROUP)]
        mapped = [wide(nt(c_w[h], b_w[h]) * SCALE) for h in heads]
        read = [halves(nn(qh[h], m)) for h, m in zip(heads, mapped)]
        score = [nt(wide(r), kown[...]) for r in read]
        causal = place(iota((ROWS, ROWS), 1)) <= place(iota((ROWS, ROWS), 0))
        mixed = []
        for h, r, s in zip(heads, read, score):
            t_all[h] = r
            s_all[h] = s
            gap = twice(rcol[h], 1) - rows[0, pl.ds(h, 1), :]
            decay = jnp.where(causal, jnp.exp(gap), 0.0) * rows[1, pl.ds(h, 1), :]
            d_all[h] = decay
            high, low = split(s * decay)
            value = vown[:, :DIM]
            mixed.append(nn(high, value) + nn(low, value) + jnp.exp(rcol[h]) * product(r, mom[h]))
        flats = [nn(wide(m), twice(x_w[h], 0)) for h, m in zip(heads, mixed)]
        for h, m, flat in zip(heads, mixed, flats):
            z_all[h] = m
            y_all[h] = flat
            taught = tq[h].astype(F32)
            scaled = flat * gains[pl.ds(h, 1), :]
            stats[0] += flat * flat
            stats[1] += taught * taught
            stats[2] += scaled * scaled
            stats[3] += scaled * taught

    each(HEADS // GROUP, forward)

    lane = iota((ROWS, DIM), 1)
    packed = jnp.zeros((ROWS, DIM), F32)
    for index in range(4):
        packed = jnp.where(lane == index, jnp.sum(stats[index], axis=1, keepdims=True), packed)
    stx[tp] = packed.T[:8]

    def t_copy(peer, slot):
        return remote(stx.at[slot], stx.at[slot], t_ss.at[peer], t_rs.at[slot], {"tp": peer})

    others(TP, tp, lambda peer: t_copy(peer, tp).start())
    tangents(0)
    for piece in range(1, PIECES):

        @pl.when(needs(chip, piece))
        def _(piece=piece):
            tangents(piece)

    others(TP, tp, lambda peer: t_copy(peer, peer).wait_recv())
    sums = jnp.sum(stx[...], axis=0)
    inverse = lax.rsqrt(sums[0:1] / FEATURES + EPS)
    inverse_t = lax.rsqrt(sums[1:2] / FEATURES + EPS)
    cross = (2.0 / TOKENS) * (inverse * sums[2:3] - inverse_t * sums[3:4])
    pull = inverse * inverse * inverse * cross / FEATURES
    line = iota((8, ROWS), 0)
    spread = columns_of(jnp.where(line == 0, inverse, jnp.where(line == 1, inverse_t, pull)))
    for index in range(3):
        cols[index] = jnp.broadcast_to(spread[:, index : index + 1], (ROWS, DIM))

    def sib_copy(head):
        return remote(gbuf.at[1 - core, head], sibr.at[head], sib_ss.at[head], sib_rs.at[head], {"ctx": sibling})

    def r_copy(head, slot):
        return remote(pairsum.at[head], rs.at[slot], r_ss.at[head], r_rs.at[slot], {"ctx": 2 * head + core})

    def pass_on(group):
        for index in range(GROUP):
            head = GROUP * group + index
            sib_copy(head).wait_recv()
            pairsum[head] = gbuf[core, head] + sibr[head]

            @pl.when(head != chip)
            def _(head=head):
                r_copy(head, chip).start()

            @pl.when(head == chip)
            def _(head=head):
                rs[chip] = pairsum[head]

    def backward(group):
        heads = [GROUP * group + index for index in range(GROUP)]
        d_flats, small = [], []
        order = jnp.where(iota((ROWS, ROWS), 0) == place(iota((ROWS, ROWS), 1)), 1.0, 0.0).astype(BF16)
        for h in heads:
            flat = y_all[h]
            gain = gains[pl.ds(h, 1), :]
            inv = cols[0]
            unit = flat * inv
            normed = unit * gain
            out[:, pl.ds(pl.multiple_of(h * DIM, DIM), DIM)] = nn(order, normed.astype(BF16)).astype(BF16)
            d_normed = (2.0 / TOKENS) * (normed - tq[h].astype(F32) * cols[1])
            d_flat = d_normed * gain * inv - flat * cols[2]
            d_flats.append(d_flat)
            moved = d_flat * flat
            small.append([
                jnp.sum(d_normed * unit, axis=0, keepdims=True),
                jnp.sum(moved * rcol[h], axis=0, keepdims=True),
                jnp.sum(moved * rbcol[h], axis=0, keepdims=True),
            ])
        d_mixed = [nt(wide(d), twice(x_w[h], 1)) for h, d in zip(heads, d_flats)]
        d_score = [nt(wide(d), vown[...]) * d_all[h] for h, d in zip(heads, d_mixed)]
        for h, d in zip(heads, d_flats):
            gbuf[1, h, :DIM] = product(z_all[h].T, d)
        d_read = []
        for index, h in enumerate(heads):
            felt = jnp.sum(d_score[index] * s_all[h], axis=0, keepdims=True)
            from_decay = felt * rows[0, pl.ds(h, 1), :]
            from_bias = felt * (rows[3, pl.ds(h, 1), :] - rows[2, pl.ds(h, 1), :])
            high, low = split(d_score[index])
            key = kown[:, :DIM]
            d_late = jnp.exp(rcol[h]) * d_mixed[index]
            d_read.append(nn(high, key) + nn(low, key) + product_t(d_late, mom[h]))
            d_state = product(t_all[h].T, d_late)
            small[index][1] += jnp.sum(d_state * tangent[h, :DIM], axis=0, keepdims=True) - halves(from_decay)
            small[index][2] += jnp.sum(d_state * tangent[h, DIM:], axis=0, keepdims=True) + halves(from_bias)
        tail = iota((TAIL, DIM), 0)
        for index, h in enumerate(heads):
            query_t = qh[h].astype(F32).T.astype(BF16)
            gbuf[0, h, :DIM] = halves(nn(query_t, wide(d_read[index])))
            lines = jnp.zeros((TAIL, DIM), F32)
            for line, value in enumerate(small[index]):
                lines = jnp.where(tail == line, value, lines)
            gbuf[0, h, DIM:] = jnp.zeros((TAIL, DIM), F32)
            gbuf[1, h, DIM:] = lines
            sib_copy(h).start()

        @pl.when(group > 0)
        def _():
            pass_on(group - 1)

    each(HEADS // GROUP, backward)
    out_copy = pltpu.make_async_copy(out, out_to, out_sem.at[0])
    out_copy.start()
    pass_on(HEADS // GROUP - 1)

    others(CHIPS, chip, lambda peer: r_copy(peer, peer).wait_recv())
    fin[core, chip] = jnp.sum(rs[...], axis=0)

    def ag_copy(peer, slot):
        held = fin.at[core, slot]
        return remote(held, held, ag_ss.at[peer], ag_rs.at[slot], {"ctx": 2 * peer + core})

    def fw_copy(slot, side):
        held = fin.at[side, slot]
        return remote(held, held, fw_ss.at[slot], fw_rs.at[slot], {"ctx": sibling})

    others(CHIPS, chip, lambda peer: ag_copy(peer, chip).start())
    fw_copy(chip, core).start()

    def hand_over(peer):
        ag_copy(peer, peer).wait_recv()
        fw_copy(peer, core).start()

    others(CHIPS, chip, hand_over)
    for head in range(HEADS):
        fw_copy(head, 1 - core).wait_recv()
    fin_copy = pltpu.make_async_copy(fin, fin_to, out_sem.at[1])
    fin_copy.start()

    others(CTX, me, lambda peer: q_copy(peer, me).wait_send())
    for piece in range(PIECES):

        def left(peer, piece=piece):
            @pl.when(needs(peer, piece))
            def _():
                kv_copy(peer, chip, piece).wait_send()

        others(CHIPS, chip, left)

        @pl.when(needs(chip, piece))
        def _(piece=piece):
            for slot in range(CHIPS):
                kf_copy(slot, core, piece).wait_send()

    others(TP, tp, lambda peer: t_copy(peer, tp).wait_send())
    others(CHIPS, chip, lambda peer: r_copy(peer, chip).wait_send())
    others(CHIPS, chip, lambda peer: ag_copy(peer, chip).wait_send())
    for head in range(HEADS):
        sib_copy(head).wait_send()
        fw_copy(head, core).wait_send()
    out_copy.wait()
    fin_copy.wait()


def closing(out_in, fin, c_w, b_w, out, grad_c, grad_b, grad_x, grad_decay, grad_bias, grad_gain):
    out[...] = out_in[...]
    for head in range(HEADS):
        grad_x[head] = fin[1, head, :DIM]
        joint = fin[0, head, :DIM]
        grad_c[head] = nn(wide(joint), twice(b_w[head], 0)) * SCALE
        grad_b[head] = nn(wide(joint.T), twice(c_w[head], 0)) * SCALE
        grad_gain[head * DIM : (head + 1) * DIM] = fin[1, head, DIM]
        grad_decay[head] = jnp.sum(fin[1, head, DIM + 1])
        grad_bias[head] = jnp.sum(fin[1, head, DIM + 2])


def local(queries, keys, values, dt_logits, decay_log, dt_bias, c_weight, b_weight, x_weight, norm_gain):
    whole = pl.BlockSpec(memory_space=pltpu.VMEM)
    there = pl.BlockSpec(memory_space=pl.ANY)
    scalars = pl.BlockSpec(memory_space=pltpu.SMEM)
    dma = pltpu.SemaphoreType.DMA

    def f32(*shape):
        return pltpu.VMEM(shape, F32)

    def bf16(*shape):
        return pltpu.VMEM(shape, BF16)

    square = (HEADS, DIM, DIM)
    by_row = (HEADS, ROWS, DIM)
    message = (DIM + TAIL, DIM)
    out, fin = pl.pallas_call(
        kernel,
        out_shape=(
            jax.ShapeDtypeStruct((ROWS, HEADS * DIM), BF16),
            jax.ShapeDtypeStruct((2, HEADS, *message), F32),
        ),
        in_specs=[there] * 3 + [whole] + [scalars] * 2 + [there] * 3 + [whole],
        out_specs=[there] * 2,
        scratch_shapes=[
            bf16(CTX, SUB, HEADS * DIM),
            bf16(CTX, HEAD_ROWS + ROWS, 2 * DIM),
            bf16(CTX, ROWS, DIM),
            bf16(CTX, ROWS, 2 * DIM),
            bf16(*by_row),
            f32(ROWS, WIDTH * ROWS),
            f32(HEADS, ROWS, 2 * DIM),
            f32(*by_row),
            bf16(*by_row),
            f32(*square),
            f32(HEADS, 2 * DIM, DIM),
            f32(3, PIECES, HEADS, CTX * PIECE),
            f32(4, HEADS, ROWS),
            f32(*by_row),
            f32(*by_row),
            bf16(ROWS, 2 * DIM),
            bf16(ROWS, 2 * DIM),
            f32(HEADS, DIM),
            bf16(*square),
            bf16(*square),
            bf16(*square),
            f32(*by_row),
            f32(HEADS, ROWS, ROWS),
            f32(HEADS, ROWS, ROWS),
            f32(*by_row),
            f32(*by_row),
            f32(4, ROWS, DIM),
            f32(TP, 8, ROWS),
            f32(3, ROWS, DIM),
            bf16(ROWS, HEADS * DIM),
            f32(2, HEADS, *message),
            f32(HEADS, *message),
            f32(HEADS, *message),
            f32(CHIPS, *message),
            f32(2, HEADS, *message),
            dma((3,)), dma((3,)), dma((2,)),
            dma((CTX,)), dma((CTX,)),
            dma((CHIPS, PIECES)), dma((CHIPS, PIECES)), dma((CHIPS, PIECES)), dma((CHIPS, PIECES)),
            dma((TP,)), dma((TP,)),
            dma((HEADS,)), dma((HEADS,)), dma((CHIPS,)), dma((CHIPS,)),
            dma((CHIPS,)), dma((CHIPS,)), dma((HEADS,)), dma((HEADS,)),
        ],
        compiler_params=pltpu.CompilerParams(
            collective_id=0, has_side_effects=True, vmem_limit_bytes=56 * 2**20
        ),
    )(queries, keys, values, dt_logits, decay_log, dt_bias, c_weight, b_weight, x_weight, norm_gain)
    return pl.pallas_call(
        closing,
        out_shape=(
            jax.ShapeDtypeStruct((ROWS, HEADS * DIM), BF16),
            jax.ShapeDtypeStruct(square, F32),
            jax.ShapeDtypeStruct(square, F32),
            jax.ShapeDtypeStruct(square, F32),
            jax.ShapeDtypeStruct((HEADS,), F32),
            jax.ShapeDtypeStruct((HEADS,), F32),
            jax.ShapeDtypeStruct((HEADS * DIM,), F32),
        ),
        in_specs=[whole] * 4,
        out_specs=[whole] * 4 + [scalars] * 2 + [whole],
        compiler_params=pltpu.CompilerParams(vmem_limit_bytes=32 * 2**20),
    )(out, fin, c_weight, b_weight)


def solution(mesh):
    return jax.shard_map(
        local,
        mesh=mesh,
        in_specs=(
            P("ctx", "tp"),
            P("ctx", "tp"),
            P("ctx", "tp"),
            P("ctx", "tp"),
            P("tp"),
            P("tp"),
            P("tp", None, None),
            P("tp", None, None),
            P("tp", None, None),
            P("tp"),
        ),
        out_specs=(
            P("ctx", "tp"),
            P("tp", None, None),
            P("tp", None, None),
            P("tp", None, None),
            P("tp"),
            P("tp"),
            P("tp"),
        ),
        check_vma=False,
    )
```

```python
import jax
import jax.numpy as jnp
from jax import lax
from jax.experimental import pallas as pl
from jax.experimental.pallas import tpu as pltpu
from jax.sharding import PartitionSpec as P

MESH = pl.DeviceIdType.MESH
F32 = jnp.float32
BF16 = jnp.bfloat16
HEADS = 8
DIM = 128
ROWS = 256
CTX = 16
TP = 8
CHIPS = CTX // 2
SUB = ROWS // CTX
PIECES = 2
PIECE = ROWS // PIECES
WIDTH = 4
STEPS = CTX // PIECES // WIDTH
QUAD = 4
HEAD_ROWS = 16
TAIL = 8
GROUP = 2
TOKENS = ROWS * CTX
FEATURES = HEADS * DIM * TP
EPS = 1e-05
SCALE = DIM**-0.5
LOG2E = 1.4426950408889634
NEG = -1e30
ORDER = (0, 2, 5, 7, 1, 3, 4, 6)


def nn(a, b):
    return lax.dot_general(a, b, (((1,), (0,)), ((), ())), preferred_element_type=F32)


def nt(a, b):
    return lax.dot_general(a, b, (((1,), (1,)), ((), ())), preferred_element_type=F32)


def split(value):
    high = value.astype(BF16)
    return high, (value - high.astype(F32)).astype(BF16)


def wide(value):
    return jnp.concatenate(split(value), axis=1)


def twice(value, axis):
    return jnp.concatenate([value, value], axis=axis)


def halves(value):
    return value[:, :DIM] + value[:, DIM:]


def by_mask(value, mask):
    first = value.astype(BF16)
    rest = value - first.astype(F32)
    second = rest.astype(BF16)
    third = (rest - second.astype(F32)).astype(BF16)
    return nn(first, mask) + nn(second, mask) + nn(third, mask)


def product(a, b):
    a_high, a_low = split(a)
    b_high, b_low = split(b)
    return halves(nn(a_high, jnp.concatenate([b_high, b_low], axis=1))) + nn(a_low, b_high)


def product_t(a, b):
    a_high, a_low = split(a)
    b_high, b_low = split(b)
    return nt(jnp.concatenate([a_high, a_low], axis=1), twice(b_high, 1)) + nt(a_high, b_low)


def iota(shape, axis):
    return lax.broadcasted_iota(jnp.int32, shape, axis)


def place(row):
    return (row & 15) * 16 + (row >> 4)


def columns_of(rows):
    return jnp.concatenate([rows, jnp.zeros((DIM - 8, ROWS), F32)], axis=0).T


def steps_of(logits, bias):
    raised = logits + bias
    faded = jnp.exp(-jnp.abs(raised))
    step = jnp.maximum(raised, 0.0) + jnp.log1p(faded)
    slope = jnp.where(raised >= 0.0, 1.0, faded) / (1.0 + faded)
    return step, slope


def kernel(
    q_in, k_in, v_in, z_hbm, decay_hbm, bias_hbm, c_in, b_in, x_in, gain_hbm,
    out_to, fin_to,
    qr, kv, kpos, vpos, qh, hide, acc, top, tq, mom, tangent, wts, rows, rcol, rbcol, kown, vown, gains, both_maps,
    c_w, b_w, x_w, t_all, s_all, d_all, z_all, y_all, stats, stx, cols, out,
    gbuf, sibr, pairsum, rs, fin,
    z_in, decay_in, bias_in, gain_in,
    local_sem, w_sem, out_sem, fin_sem, q_ss, q_rs, kv_ss, kv_rs, kf_ss, kf_rs, t_ss, t_rs, sib_ss, sib_rs, r_ss, r_rs,
    ag_ss, ag_rs, fw_ss, fw_rs,
):
    me = lax.axis_index("ctx")
    tp = lax.axis_index("tp")
    core = lax.rem(me, 2)
    chip = me // 2
    sibling = me + 1 - 2 * core

    def remote(src, dst, send, recv, where):
        return pltpu.make_async_remote_copy(
            src_ref=src, dst_ref=dst, send_sem=send, recv_sem=recv, device_id=where, device_id_type=MESH
        )

    def others(count, mine, body):
        for step in range(1, count):
            body((mine + step) & (count - 1))

    def each(count, body):
        def one(step, carry):
            body(step)
            return carry

        lax.fori_loop(0, count, one, 0)

    own_rows = pl.ds(pl.multiple_of(SUB * me, SUB), SUB)
    body_rows = pl.ds(HEAD_ROWS, ROWS)
    own = [
        pltpu.make_async_copy(k_in, kv.at[me, body_rows, pl.ds(0, DIM)], local_sem.at[0]),
        pltpu.make_async_copy(v_in, kv.at[me, body_rows, pl.ds(DIM, DIM)], local_sem.at[1]),
        pltpu.make_async_copy(q_in.at[own_rows], qr.at[me], local_sem.at[2]),
    ]
    few = [
        pltpu.make_async_copy(z_hbm, z_in, local_sem.at[3]),
        pltpu.make_async_copy(decay_hbm, decay_in, local_sem.at[4]),
        pltpu.make_async_copy(bias_hbm, bias_in, local_sem.at[5]),
        pltpu.make_async_copy(gain_hbm, gain_in, local_sem.at[6]),
    ]
    for copy in few:
        copy.start()
    for copy in own:
        copy.start()
    weights = [
        pltpu.make_async_copy(c_in, c_w, w_sem.at[0]),
        pltpu.make_async_copy(b_in, b_w, w_sem.at[1]),
        pltpu.make_async_copy(x_in, x_w, w_sem.at[2]),
    ]
    for copy in weights:
        copy.start()
    barrier = pltpu.get_barrier_semaphore()
    others(CTX, me, lambda peer: pl.semaphore_signal(barrier, inc=1, device_id={"ctx": peer}, device_id_type=MESH))
    others(TP, tp, lambda peer: pl.semaphore_signal(barrier, inc=1, device_id={"tp": peer}, device_id_type=MESH))
    for copy in few:
        copy.wait()
    own_z = z_in[...].astype(F32)
    kv[me, :HEAD_ROWS, :] = jnp.concatenate([own_z, jnp.zeros_like(own_z)], axis=0).astype(BF16)
    for head in range(HEADS):
        gains[head : head + 1, :] = gain_in[head * DIM : (head + 1) * DIM].reshape(1, DIM)
        acc[head] = jnp.zeros((ROWS, 2 * DIM), F32)
        top[head] = jnp.full((ROWS, DIM), NEG, F32)
    mom[...] = jnp.zeros_like(mom)
    tangent[...] = jnp.zeros_like(tangent)
    stats[...] = jnp.zeros_like(stats)
    last = me // WIDTH
    shown = (ROWS, WIDTH * ROWS)
    key_place = place(iota(shown, 1) & (ROWS - 1)) + (iota(shown, 1) >> 8) * ROWS + WIDTH * ROWS * last
    hide[...] = jnp.where(key_place <= place(iota(shown, 0)) + ROWS * me, 0.0, NEG)
    head_line = iota((HEADS, ROWS), 0)
    decay_rate = jnp.zeros((HEADS, ROWS), F32)
    bias = jnp.zeros((HEADS, ROWS), F32)
    for head in range(HEADS):
        decay_rate = jnp.where(head_line == head, decay_in[head], decay_rate)
        bias = jnp.where(head_line == head, bias_in[head], bias)
    speed = -jnp.exp(decay_rate)
    for copy in weights[:2]:
        copy.wait()
    for head in range(HEADS):
        both_maps[head] = wide(nt(c_w[head], b_w[head]) * SCALE)
    for copy in own:
        copy.wait()
    pl.semaphore_wait(barrier, CTX - 1 + TP - 1)

    def part_of(piece):
        if piece == 0:
            return pl.ds(0, HEAD_ROWS + PIECE)
        return pl.ds(HEAD_ROWS + PIECE * piece, PIECE)

    def kv_copy(peer, slot, piece):
        held = kv.at[2 * slot + core, part_of(piece)]
        return remote(held, held, kv_ss.at[peer, piece], kv_rs.at[slot, piece], {"ctx": 2 * peer + core})

    def kf_copy(slot, side, piece):
        held = kv.at[2 * slot + side, part_of(piece)]
        return remote(held, held, kf_ss.at[slot, piece], kf_rs.at[slot, piece], {"ctx": sibling})

    def needs(peer, piece):
        return peer >= piece * (CHIPS // PIECES)

    def q_copy(peer, slot):
        taken = pl.ds(pl.multiple_of(SUB * peer, SUB), SUB)
        return remote(q_in.at[taken], qr.at[slot], q_ss.at[peer], q_rs.at[slot], {"ctx": peer})

    def send_piece(piece):
        def send(peer):
            @pl.when(needs(peer, piece))
            def _():
                kv_copy(peer, chip, piece).start()

        others(CHIPS, chip, send)

        @pl.when(needs(chip, piece))
        def _():
            kf_copy(chip, core, piece).start()

    def relay(piece):
        def one(peer):
            kv_copy(peer, peer, piece).wait_recv()
            kf_copy(peer, core, piece).start()

        others(CHIPS, chip, one)

    def arrived(piece):
        kf_copy(chip, 1 - core, piece).wait_recv()
        others(CHIPS, chip, lambda peer: kf_copy(peer, 1 - core, piece).wait_recv())

    send_piece(0)
    others(CTX, me, lambda peer: q_copy(peer, me).start())
    for piece in range(1, PIECES):
        send_piece(piece)

    relay(0)
    arrived(0)

    logits = kv[:, :HEAD_ROWS, :].astype(F32)[:, :HEADS, :]
    step, slope = steps_of(logits, bias[None])
    rate = speed[None] * step
    rate_b = speed[None] * slope
    lower = iota((ROWS, ROWS), 0)
    upper = iota((ROWS, ROWS), 1)
    after = jnp.where((lower > upper) & (lower < SUB * me), 1.0, 0.0).astype(BF16)
    span = by_mask(jnp.sum(rate, axis=0), after)
    span_b = by_mask(jnp.sum(rate_b, axis=0), after)
    earlier = iota((HEADS, ROWS), 1) < SUB * me
    for source in reversed(range(CTX)):
        weight = jnp.where(earlier, jnp.exp(span) * step[source], 0.0)
        kinds = (weight, weight * span, weight * (span_b + slope[source] / step[source]))
        for index, kind in enumerate(kinds):
            for piece in range(PIECES):
                wts[index, piece, :, source * PIECE : (source + 1) * PIECE] = kind[:, piece * PIECE : (piece + 1) * PIECE]
        span = span + rate[source]
        span_b = span_b + rate_b[source]

    pick = jnp.where(lower == SUB * me + (upper & 15), 1.0, 0.0).astype(BF16)
    picked = nn(logits.reshape(CTX * HEADS, ROWS).astype(BF16), pick).reshape(CTX, HEADS, ROWS)
    matched = iota((CTX, HEADS, ROWS), 0) == (iota((CTX, HEADS, ROWS), 2) >> 4)
    own_logits = jnp.sum(jnp.where(matched, picked, 0.0), axis=0)
    own_step, own_slope = steps_of(own_logits, bias)
    until = jnp.where(place(lower) <= place(upper), 1.0, 0.0).astype(BF16)
    running = by_mask(speed * own_step, until)
    running_b = by_mask(speed * own_slope, until)
    rows[0] = running
    rows[1] = own_step
    rows[2] = running_b
    rows[3] = own_slope / own_step
    running_c = columns_of(running)
    running_bc = columns_of(running_b)
    for head in range(HEADS):
        rcol[head] = jnp.broadcast_to(running_c[:, head : head + 1], (ROWS, DIM))
        rbcol[head] = jnp.broadcast_to(running_bc[:, head : head + 1], (ROWS, DIM))

    def gathered(piece, quad):
        part = kv[pl.ds(QUAD * quad, QUAD), pl.ds(HEAD_ROWS + PIECE * piece, PIECE), :]
        both = part.reshape(QUAD * PIECE, 2 * DIM)
        lanes = pl.ds(pl.multiple_of(quad * QUAD * PIECE, QUAD * PIECE), QUAD * PIECE)
        return both[:, :DIM].astype(F32).T, both[:, DIM:], lanes

    def moments(piece):
        def one(quad):
            key_t, value, lanes = gathered(piece, quad)
            double = twice(value, 0)
            for head in range(HEADS):
                mom[head] += nn(wide(key_t * wts[0, piece, head : head + 1, lanes]), double)

        each(CTX // QUAD, one)

    def tangents(piece):
        def one(quad):
            key_t, value, lanes = gathered(piece, quad)
            for head in range(HEADS):
                by_decay = (key_t * wts[1, piece, head : head + 1, lanes]).astype(BF16)
                by_bias = (key_t * wts[2, piece, head : head + 1, lanes]).astype(BF16)
                tangent[head] += nn(jnp.concatenate([by_decay, by_bias], axis=0), value)

        each(CTX // QUAD, one)

    def sort(piece):
        def one(index):
            block = piece * (CTX // PIECES) + index
            part = pl.ds(pl.multiple_of(HEAD_ROWS + SUB * block, SUB), SUB)
            both = kv[:, part, :].reshape(ROWS, 2 * DIM)
            kpos[block] = both[:, :DIM]
            vpos[block, :, :DIM] = both[:, DIM:]
            vpos[block, :, DIM:] = jnp.ones((ROWS, DIM), BF16)

        each(CTX // PIECES, one)

    def attend(chunk, masked):
        blocks = pl.ds(WIDTH * chunk, WIDTH)
        key = kpos[blocks].reshape(WIDTH * ROWS, DIM)
        value = vpos[blocks].reshape(WIDTH * ROWS, 2 * DIM)

        def mix(head, weights, shrink):
            acc[head] = acc[head] * twice(shrink, 1) + nn(weights, value)

        scores = nt(qh[0], key)
        waiting = None
        for head in range(HEADS):
            following = nt(qh[head + 1], key) if head + 1 < HEADS else None
            if masked:
                scores = scores + hide[...]
            old = top[head]
            new = jnp.maximum(old, jnp.max(scores, axis=1, keepdims=True))
            weights = jnp.exp2((scores - new[:, :1]) * (SCALE * LOG2E)).astype(BF16)
            shrink = jnp.exp2((old - new) * (SCALE * LOG2E))
            top[head] = new
            if waiting is not None:
                mix(*waiting)
            waiting = (head, weights, shrink)
            scores = following
        mix(*waiting)

    sort(0)
    moments(0)
    others(CTX, me, lambda peer: q_copy(peer, peer).wait_recv())
    for head in range(HEADS):
        qh[head] = qr[:, :, head * DIM : (head + 1) * DIM].reshape(ROWS, DIM)

    def teach(chunk, carry):
        attend(chunk, False)
        for piece in range(1, PIECES):

            @pl.when(needs(chip, piece) & (chunk == STEPS * piece - 2))
            def _(piece=piece):
                relay(piece)

            @pl.when(needs(chip, piece) & (chunk == STEPS * piece - 1))
            def _(piece=piece):
                arrived(piece)
                sort(piece)
                moments(piece)

        return carry

    lax.fori_loop(0, last, teach, 0)
    attend(last, True)

    def close(head):
        total = acc[head]
        tq[head] = (total[:, :DIM] / total[:, DIM:]).astype(BF16)

    each(HEADS, close)

    weights[2].wait()
    own_kv = kv[:, pl.ds(pl.multiple_of(HEAD_ROWS + SUB * me, SUB), SUB), :].reshape(ROWS, 2 * DIM)
    kown[...] = twice(own_kv[:, :DIM], 1)
    vown[...] = twice(own_kv[:, DIM:], 1)

    def forward(group):
        heads = [GROUP * group + index for index in range(GROUP)]
        read = [halves(nn(qh[h], both_maps[h])) for h in heads]
        score = [nt(wide(r), kown[...]) for r in read]
        causal = place(iota((ROWS, ROWS), 1)) <= place(iota((ROWS, ROWS), 0))
        mixed = []
        for h, r, s in zip(heads, read, score):
            t_all[h] = r
            s_all[h] = s
            gap = twice(rcol[h], 1) - rows[0, pl.ds(h, 1), :]
            decay = jnp.where(causal, jnp.exp(gap), 0.0) * rows[1, pl.ds(h, 1), :]
            d_all[h] = decay
            high, low = split(s * decay)
            value = vown[:, :DIM]
            mixed.append(nn(high, value) + nn(low, value) + jnp.exp(rcol[h]) * product(r, mom[h]))
        flats = [nn(wide(m), twice(x_w[h], 0)) for h, m in zip(heads, mixed)]
        for h, m, flat in zip(heads, mixed, flats):
            z_all[h] = m
            y_all[h] = flat
            taught = tq[h].astype(F32)
            scaled = flat * gains[pl.ds(h, 1), :]
            stats[0] += flat * flat
            stats[1] += taught * taught
            stats[2] += scaled * scaled
            stats[3] += scaled * taught

    each(HEADS // GROUP, forward)

    lane = iota((ROWS, DIM), 1)
    packed = jnp.zeros((ROWS, DIM), F32)
    for index in range(4):
        packed = jnp.where(lane == index, jnp.sum(stats[index], axis=1, keepdims=True), packed)
    stx[tp] = packed.T[:8]

    def t_copy(peer, slot):
        return remote(stx.at[slot], stx.at[slot], t_ss.at[peer], t_rs.at[slot], {"tp": peer})

    others(TP, tp, lambda peer: t_copy(peer, tp).start())
    tangents(0)
    for piece in range(1, PIECES):

        @pl.when(needs(chip, piece))
        def _(piece=piece):
            tangents(piece)

    others(TP, tp, lambda peer: t_copy(peer, peer).wait_recv())
    sums = jnp.sum(stx[...], axis=0)
    inverse = lax.rsqrt(sums[0:1] / FEATURES + EPS)
    inverse_t = lax.rsqrt(sums[1:2] / FEATURES + EPS)
    cross = (2.0 / TOKENS) * (inverse * sums[2:3] - inverse_t * sums[3:4])
    pull = inverse * inverse * inverse * cross / FEATURES
    line = iota((8, ROWS), 0)
    spread = columns_of(jnp.where(line == 0, inverse, jnp.where(line == 1, inverse_t, pull)))
    for index in range(3):
        cols[index] = jnp.broadcast_to(spread[:, index : index + 1], (ROWS, DIM))

    def sib_copy(group):
        part = pl.ds(GROUP * group, GROUP)
        return remote(gbuf.at[1 - core, part], sibr.at[part], sib_ss.at[group], sib_rs.at[group], {"ctx": sibling})

    def r_copy(turn, head, slot):
        return remote(pairsum.at[turn], rs.at[slot], r_ss.at[head], r_rs.at[slot], {"ctx": 2 * head + core})

    def turns(group):
        heads = []
        for index in range(GROUP):
            turn = GROUP * group + index
            owner = (chip + turn) & 3
            first = (owner >> 1) * 5 + (owner & 1) * 2
            heads.append(jnp.where(turn < HEADS // 2, first, first + 1 - 2 * (first & 1)))
        return heads

    def order_of(head):
        if isinstance(head, int):
            return ORDER.index(head)
        late = (head + (head >> 2)) & 1
        return 4 * late + 2 * (head >> 2) + ((head & 3) >> 1)

    def pass_on(group):
        sib_copy(group).wait_recv()
        for index, head in enumerate(turns(group)):
            turn = GROUP * group + index
            pairsum[turn] = gbuf[core, turn] + sibr[turn]

            @pl.when(head != chip)
            def _(head=head, turn=turn):
                r_copy(turn, head, chip).start()

            @pl.when(head == chip)
            def _(turn=turn):
                rs[chip] = pairsum[turn]

    def backward(group):
        heads = turns(group)
        d_flats, small = [], []
        order = jnp.where(iota((ROWS, ROWS), 0) == place(iota((ROWS, ROWS), 1)), 1.0, 0.0).astype(BF16)
        for h in heads:
            flat = y_all[h]
            gain = gains[pl.ds(h, 1), :]
            inv = cols[0]
            unit = flat * inv
            normed = unit * gain
            out[:, pl.ds(pl.multiple_of(h * DIM, DIM), DIM)] = nn(order, normed.astype(BF16)).astype(BF16)
            d_normed = (2.0 / TOKENS) * (normed - tq[h].astype(F32) * cols[1])
            d_flat = d_normed * gain * inv - flat * cols[2]
            d_flats.append(d_flat)
            moved = d_flat * flat
            small.append([
                jnp.sum(d_normed * unit, axis=0, keepdims=True),
                jnp.sum(moved * rcol[h], axis=0, keepdims=True),
                jnp.sum(moved * rbcol[h], axis=0, keepdims=True),
            ])
        d_mixed = [nt(wide(d), twice(x_w[h], 1)) for h, d in zip(heads, d_flats)]
        d_score = [nt(wide(d), vown[...]) * d_all[h] for h, d in zip(heads, d_mixed)]
        for index, h in enumerate(heads):
            gbuf[1, GROUP * group + index, :DIM] = product(z_all[h].T, d_flats[index])
        d_read = []
        for index, h in enumerate(heads):
            felt = jnp.sum(d_score[index] * s_all[h], axis=0, keepdims=True)
            from_decay = felt * rows[0, pl.ds(h, 1), :]
            from_bias = felt * (rows[3, pl.ds(h, 1), :] - rows[2, pl.ds(h, 1), :])
            high, low = split(d_score[index])
            key = kown[:, :DIM]
            d_late = jnp.exp(rcol[h]) * d_mixed[index]
            d_read.append(nn(high, key) + nn(low, key) + product_t(d_late, mom[h]))
            d_state = product(t_all[h].T, d_late)
            small[index][1] += jnp.sum(d_state * tangent[h, :DIM], axis=0, keepdims=True) - halves(from_decay)
            small[index][2] += jnp.sum(d_state * tangent[h, DIM:], axis=0, keepdims=True) + halves(from_bias)
        tail = iota((TAIL, DIM), 0)
        for index, h in enumerate(heads):
            query_t = qh[h].astype(F32).T.astype(BF16)
            turn = GROUP * group + index
            gbuf[0, turn, :DIM] = halves(nn(query_t, wide(d_read[index])))
            lines = jnp.zeros((TAIL, DIM), F32)
            for line, value in enumerate(small[index]):
                lines = jnp.where(tail == line, value, lines)
            gbuf[0, turn, DIM:] = jnp.zeros((TAIL, DIM), F32)
            gbuf[1, turn, DIM:] = lines
        sib_copy(group).start()

        @pl.when(group > 0)
        def _():
            pass_on(group - 1)

    each(HEADS // GROUP, backward)
    out_copy = pltpu.make_async_copy(out, out_to, out_sem.at[0])
    out_copy.start()
    pass_on(HEADS // GROUP - 1)

    others(CHIPS, chip, lambda peer: r_copy(0, peer, peer).wait_recv())
    fin[core, order_of(chip)] = jnp.sum(rs[...], axis=0)

    def ag_copy(peer, slot):
        held = fin.at[core, order_of(slot)]
        return remote(held, held, ag_ss.at[peer], ag_rs.at[slot], {"ctx": 2 * peer + core})

    def fw_copy(half, side):
        held = fin.at[side, pl.ds(half * (CHIPS // 2), CHIPS // 2)]
        return remote(held, held, fw_ss.at[half], fw_rs.at[half], {"ctx": sibling})

    def fin_copy(half):
        part = pl.ds(half * (CHIPS // 2), CHIPS // 2)
        return pltpu.make_async_copy(fin.at[:, part], fin_to.at[:, part], fin_sem.at[half])

    others(CHIPS, chip, lambda peer: ag_copy(peer, chip).start())
    for half in range(2):
        for head in ORDER[half * (CHIPS // 2) : (half + 1) * (CHIPS // 2)]:

            @pl.when(chip != head)
            def _(head=head):
                ag_copy(head, head).wait_recv()

        fw_copy(half, core).start()
    for half in range(2):
        fw_copy(half, 1 - core).wait_recv()
        fin_copy(half).start()

    others(CTX, me, lambda peer: q_copy(peer, me).wait_send())
    for piece in range(PIECES):

        def left(peer, piece=piece):
            @pl.when(needs(peer, piece))
            def _():
                kv_copy(peer, chip, piece).wait_send()

        others(CHIPS, chip, left)

        @pl.when(needs(chip, piece))
        def _(piece=piece):
            for slot in range(CHIPS):
                kf_copy(slot, core, piece).wait_send()

    others(TP, tp, lambda peer: t_copy(peer, tp).wait_send())
    others(CHIPS, chip, lambda peer: r_copy(0, peer, chip).wait_send())
    others(CHIPS, chip, lambda peer: ag_copy(peer, chip).wait_send())
    for group in range(HEADS // GROUP):
        sib_copy(group).wait_send()
    for half in range(2):
        fw_copy(half, core).wait_send()
        fin_copy(half).wait()
    out_copy.wait()


def closing(out_in, fin, c_w, b_w, out, grad_c, grad_b, grad_x, grad_decay, grad_bias, grad_gain):
    out[...] = out_in[...]
    for head in range(HEADS):
        slot = ORDER.index(head)
        grad_x[head] = fin[1, slot, :DIM]
        joint = fin[0, slot, :DIM]
        grad_c[head] = nn(wide(joint), twice(b_w[head], 0)) * SCALE
        grad_b[head] = nn(wide(joint.T), twice(c_w[head], 0)) * SCALE
        grad_gain[head * DIM : (head + 1) * DIM] = fin[1, slot, DIM]
        grad_decay[head] = jnp.sum(fin[1, slot, DIM + 1])
        grad_bias[head] = jnp.sum(fin[1, slot, DIM + 2])


def local(queries, keys, values, dt_logits, decay_log, dt_bias, c_weight, b_weight, x_weight, norm_gain):
    whole = pl.BlockSpec(memory_space=pltpu.VMEM)
    there = pl.BlockSpec(memory_space=pl.ANY)
    scalars = pl.BlockSpec(memory_space=pltpu.SMEM)
    dma = pltpu.SemaphoreType.DMA

    def f32(*shape):
        return pltpu.VMEM(shape, F32)

    def bf16(*shape):
        return pltpu.VMEM(shape, BF16)

    square = (HEADS, DIM, DIM)
    by_row = (HEADS, ROWS, DIM)
    message = (DIM + TAIL, DIM)
    arguments = (
        queries, keys, values, dt_logits.T, decay_log, dt_bias, c_weight, b_weight, x_weight, norm_gain,
    )
    given = [pltpu.with_memory_space_constraint(a, pltpu.HBM) for a in arguments]
    out, fin = pl.pallas_call(
        kernel,
        out_shape=(
            jax.ShapeDtypeStruct((ROWS, HEADS * DIM), BF16),
            jax.ShapeDtypeStruct((2, HEADS, *message), F32),
        ),
        in_specs=[pl.BlockSpec(memory_space=pltpu.HBM)] * 10,
        out_specs=[there] * 2,
        scratch_shapes=[
            bf16(CTX, SUB, HEADS * DIM),
            bf16(CTX, HEAD_ROWS + ROWS, 2 * DIM),
            bf16(CTX, ROWS, DIM),
            bf16(CTX, ROWS, 2 * DIM),
            bf16(*by_row),
            f32(ROWS, WIDTH * ROWS),
            f32(HEADS, ROWS, 2 * DIM),
            f32(*by_row),
            bf16(*by_row),
            f32(*square),
            f32(HEADS, 2 * DIM, DIM),
            f32(3, PIECES, HEADS, CTX * PIECE),
            f32(4, HEADS, ROWS),
            f32(*by_row),
            f32(*by_row),
            bf16(ROWS, 2 * DIM),
            bf16(ROWS, 2 * DIM),
            f32(HEADS, DIM),
            bf16(HEADS, DIM, 2 * DIM),
            bf16(*square),
            bf16(*square),
            bf16(*square),
            f32(*by_row),
            f32(HEADS, ROWS, ROWS),
            f32(HEADS, ROWS, ROWS),
            f32(*by_row),
            f32(*by_row),
            f32(4, ROWS, DIM),
            f32(TP, 8, ROWS),
            f32(3, ROWS, DIM),
            bf16(ROWS, HEADS * DIM),
            f32(2, HEADS, *message),
            f32(HEADS, *message),
            f32(HEADS, *message),
            f32(CHIPS, *message),
            f32(2, HEADS, *message),
            bf16(HEADS, ROWS),
            pltpu.SMEM((HEADS,), F32),
            pltpu.SMEM((HEADS,), F32),
            f32(HEADS * DIM),
            dma((7,)), dma((3,)), dma((1,)), dma((2,)),
            dma((CTX,)), dma((CTX,)),
            dma((CHIPS, PIECES)), dma((CHIPS, PIECES)), dma((CHIPS, PIECES)), dma((CHIPS, PIECES)),
            dma((TP,)), dma((TP,)),
            dma((HEADS // GROUP,)), dma((HEADS // GROUP,)), dma((CHIPS,)), dma((CHIPS,)),
            dma((CHIPS,)), dma((CHIPS,)), dma((2,)), dma((2,)),
        ],
        compiler_params=pltpu.CompilerParams(
            collective_id=0, has_side_effects=True, vmem_limit_bytes=40 * 2**20
        ),
    )(*given)
    return pl.pallas_call(
        closing,
        out_shape=(
            jax.ShapeDtypeStruct((ROWS, HEADS * DIM), BF16),
            jax.ShapeDtypeStruct(square, F32),
            jax.ShapeDtypeStruct(square, F32),
            jax.ShapeDtypeStruct(square, F32),
            jax.ShapeDtypeStruct((HEADS,), F32),
            jax.ShapeDtypeStruct((HEADS,), F32),
            jax.ShapeDtypeStruct((HEADS * DIM,), F32),
        ),
        in_specs=[whole] * 4,
        out_specs=[whole] * 4 + [scalars] * 2 + [whole],
        compiler_params=pltpu.CompilerParams(vmem_limit_bytes=16 * 2**20),
    )(out, fin, c_weight, b_weight)


def solution(mesh):
    return jax.shard_map(
        local,
        mesh=mesh,
        in_specs=(
            P("ctx", "tp"),
            P("ctx", "tp"),
            P("ctx", "tp"),
            P("ctx", "tp"),
            P("tp"),
            P("tp"),
            P("tp", None, None),
            P("tp", None, None),
            P("tp", None, None),
            P("tp"),
        ),
        out_specs=(
            P("ctx", "tp"),
            P("tp", None, None),
            P("tp", None, None),
            P("tp", None, None),
            P("tp"),
            P("tp"),
            P("tp"),
        ),
        check_vma=False,
    )
```

```python
import jax
import jax.numpy as jnp
from jax import lax
from jax.experimental import pallas as pl
from jax.experimental.pallas import tpu as pltpu
from jax.sharding import PartitionSpec as P

MESH = pl.DeviceIdType.MESH
F32 = jnp.float32
BF16 = jnp.bfloat16
HEADS = 8
DIM = 128
ROWS = 256
CTX = 16
TP = 8
CHIPS = CTX // 2
SUB = ROWS // CTX
STARTS = (0, 64, 128)
SIZES = (64, 64, 128)
PIECES = len(STARTS)
WIDTH = 4
KEYS = 512
HEAD_ROWS = 16
TAIL = 8
GROUP = 2
FORWARD = 4
TOKENS = ROWS * CTX
FEATURES = HEADS * DIM * TP
EPS = 1e-05
SCALE = DIM**-0.5
LOG2E = 1.4426950408889634
NEG = -1e30
ORDER = (0, 2, 5, 7, 1, 3, 4, 6)


def nn(a, b):
    return lax.dot_general(a, b, (((1,), (0,)), ((), ())), preferred_element_type=F32)


def nt(a, b):
    return lax.dot_general(a, b, (((1,), (1,)), ((), ())), preferred_element_type=F32)


def split(value):
    high = value.astype(BF16)
    return high, (value - high.astype(F32)).astype(BF16)


def wide(value):
    return jnp.concatenate(split(value), axis=1)


def twice(value, axis):
    return jnp.concatenate([value, value], axis=axis)


def halves(value):
    return value[:, :DIM] + value[:, DIM:]


def by_mask(value, mask):
    first = value.astype(BF16)
    rest = value - first.astype(F32)
    second = rest.astype(BF16)
    third = (rest - second.astype(F32)).astype(BF16)
    return nn(first, mask) + nn(second, mask) + nn(third, mask)


def product(a, b):
    a_high, a_low = split(a)
    b_high, b_low = split(b)
    return halves(nn(a_high, jnp.concatenate([b_high, b_low], axis=1))) + nn(a_low, b_high)


def product_t(a, b):
    a_high, a_low = split(a)
    b_high, b_low = split(b)
    return nt(jnp.concatenate([a_high, a_low], axis=1), twice(b_high, 1)) + nt(a_high, b_low)


def iota(shape, axis):
    return lax.broadcasted_iota(jnp.int32, shape, axis)


def place(row):
    return (row & 15) * 16 + (row >> 4)


def columns_of(rows):
    return jnp.concatenate([rows, jnp.zeros((DIM - 8, ROWS), F32)], axis=0).T


def steps_of(logits, bias):
    raised = logits + bias
    faded = jnp.exp(-jnp.abs(raised))
    step = jnp.maximum(raised, 0.0) + jnp.log1p(faded)
    slope = jnp.where(raised >= 0.0, 1.0, faded) / (1.0 + faded)
    return step, slope


def kernel(
    q_in, k_in, v_in, z_hbm, decay_hbm, bias_hbm, c_in, b_in, x_in, gain_hbm,
    out_to, fin_to,
    qr, kv, kpos, vpos, qh, hide, acc, top, tq, mom, tangent, wts, rows, rcol, rbcol, kown, vown, gains, both_maps,
    c_w, b_w, x_w, t_all, s_all, d_all, z_all, y_all, stats, stx, cols, out,
    gbuf, sibr, pairsum, rs, fin,
    z_in, decay_in, bias_in, gain_in,
    local_sem, w_sem, out_sem, fin_sem, q_ss, q_rs, kv_ss, kv_rs, kf_ss, kf_rs, t_ss, t_rs, sib_ss, sib_rs, r_ss, r_rs,
    ag_ss, ag_rs, fw_ss, fw_rs,
):
    me = lax.axis_index("ctx")
    tp = lax.axis_index("tp")
    core = lax.rem(me, 2)
    chip = me // 2
    sibling = me + 1 - 2 * core

    def remote(src, dst, send, recv, where):
        return pltpu.make_async_remote_copy(
            src_ref=src, dst_ref=dst, send_sem=send, recv_sem=recv, device_id=where, device_id_type=MESH
        )

    def others(count, mine, body):
        for step in range(1, count):
            body((mine + step) & (count - 1))

    def each(count, body):
        def one(step, carry):
            body(step)
            return carry

        lax.fori_loop(0, count, one, 0)

    own_rows = pl.ds(pl.multiple_of(SUB * me, SUB), SUB)
    body_rows = pl.ds(HEAD_ROWS, ROWS)
    own = [
        pltpu.make_async_copy(k_in, kv.at[me, body_rows, pl.ds(0, DIM)], local_sem.at[0]),
        pltpu.make_async_copy(v_in, kv.at[me, body_rows, pl.ds(DIM, DIM)], local_sem.at[1]),
        pltpu.make_async_copy(q_in.at[own_rows], qr.at[me], local_sem.at[2]),
    ]
    few = [
        pltpu.make_async_copy(z_hbm, z_in, local_sem.at[3]),
        pltpu.make_async_copy(decay_hbm, decay_in, local_sem.at[4]),
        pltpu.make_async_copy(bias_hbm, bias_in, local_sem.at[5]),
        pltpu.make_async_copy(gain_hbm, gain_in, local_sem.at[6]),
    ]
    for copy in few:
        copy.start()
    for copy in own:
        copy.start()
    weights = [
        pltpu.make_async_copy(c_in, c_w, w_sem.at[0]),
        pltpu.make_async_copy(b_in, b_w, w_sem.at[1]),
        pltpu.make_async_copy(x_in, x_w, w_sem.at[2]),
    ]
    for copy in weights:
        copy.start()
    barrier = pltpu.get_barrier_semaphore()
    others(CTX, me, lambda peer: pl.semaphore_signal(barrier, inc=1, device_id={"ctx": peer}, device_id_type=MESH))
    others(TP, tp, lambda peer: pl.semaphore_signal(barrier, inc=1, device_id={"tp": peer}, device_id_type=MESH))
    for copy in few:
        copy.wait()
    own_z = z_in[...].astype(F32)
    kv[me, :HEAD_ROWS, :] = jnp.concatenate([own_z, jnp.zeros_like(own_z)], axis=0).astype(BF16)
    for head in range(HEADS):
        gains[head : head + 1, :] = gain_in[head * DIM : (head + 1) * DIM].reshape(1, DIM)
        acc[head] = jnp.zeros((ROWS, 2 * DIM), F32)
        top[head] = jnp.full((ROWS, DIM), NEG, F32)
    mom[...] = jnp.zeros_like(mom)
    tangent[...] = jnp.zeros_like(tangent)
    stats[...] = jnp.zeros_like(stats)
    last = me // WIDTH
    shown = (ROWS, WIDTH * ROWS)
    key_place = place(iota(shown, 1) & (ROWS - 1)) + (iota(shown, 1) >> 8) * ROWS + WIDTH * ROWS * last
    hide[...] = jnp.where(key_place <= place(iota(shown, 0)) + ROWS * me, 0.0, NEG)
    head_line = iota((HEADS, ROWS), 0)
    decay_rate = jnp.zeros((HEADS, ROWS), F32)
    bias = jnp.zeros((HEADS, ROWS), F32)
    for head in range(HEADS):
        decay_rate = jnp.where(head_line == head, decay_in[head], decay_rate)
        bias = jnp.where(head_line == head, bias_in[head], bias)
    speed = -jnp.exp(decay_rate)
    for copy in weights[:2]:
        copy.wait()
    for head in range(HEADS):
        both_maps[head] = wide(nt(c_w[head], b_w[head]) * SCALE)
    for copy in own:
        copy.wait()
    pl.semaphore_wait(barrier, CTX - 1 + TP - 1)

    def part_of(piece):
        if piece == 0:
            return pl.ds(0, HEAD_ROWS + SIZES[0])
        return pl.ds(HEAD_ROWS + STARTS[piece], SIZES[piece])

    def kv_copy(peer, slot, piece):
        held = kv.at[2 * slot + core, part_of(piece)]
        return remote(held, held, kv_ss.at[peer, piece], kv_rs.at[slot, piece], {"ctx": 2 * peer + core})

    def kf_copy(slot, side, piece):
        held = kv.at[2 * slot + side, part_of(piece)]
        return remote(held, held, kf_ss.at[slot, piece], kf_rs.at[slot, piece], {"ctx": sibling})

    def needs(peer, piece):
        return peer >= STARTS[piece] // SUB // 2

    def q_copy(peer, slot):
        taken = pl.ds(pl.multiple_of(SUB * peer, SUB), SUB)
        return remote(q_in.at[taken], qr.at[slot], q_ss.at[peer], q_rs.at[slot], {"ctx": peer})

    def send_piece(piece):
        def send(peer):
            @pl.when(needs(peer, piece))
            def _():
                kv_copy(peer, chip, piece).start()

        others(CHIPS, chip, send)

        @pl.when(needs(chip, piece))
        def _():
            kf_copy(chip, core, piece).start()

    def relay(piece):
        def one(peer):
            kv_copy(peer, peer, piece).wait_recv()
            kf_copy(peer, core, piece).start()

        others(CHIPS, chip, one)

    def arrived(piece):
        kf_copy(chip, 1 - core, piece).wait_recv()
        others(CHIPS, chip, lambda peer: kf_copy(peer, 1 - core, piece).wait_recv())

    send_piece(0)
    others(CTX, me, lambda peer: q_copy(peer, me).start())
    for piece in range(1, PIECES):
        send_piece(piece)

    relay(0)
    arrived(0)

    logits = kv[:, :HEAD_ROWS, :].astype(F32)[:, :HEADS, :]
    step, slope = steps_of(logits, bias[None])
    rate = speed[None] * step
    rate_b = speed[None] * slope
    lower = iota((ROWS, ROWS), 0)
    upper = iota((ROWS, ROWS), 1)
    after = jnp.where((lower > upper) & (lower < SUB * me), 1.0, 0.0).astype(BF16)
    span = by_mask(jnp.sum(rate, axis=0), after)
    span_b = by_mask(jnp.sum(rate_b, axis=0), after)
    earlier = iota((HEADS, ROWS), 1) < SUB * me
    for source in reversed(range(CTX)):
        weight = jnp.where(earlier, jnp.exp(span) * step[source], 0.0)
        kinds = (weight, weight * span, weight * (span_b + slope[source] / step[source]))
        for index, kind in enumerate(kinds):
            for start, size in zip(STARTS, SIZES):
                at = CTX * start + source * size
                wts[index, :, at : at + size] = kind[:, start : start + size]
        span = span + rate[source]
        span_b = span_b + rate_b[source]

    pick = jnp.where(lower == SUB * me + (upper & 15), 1.0, 0.0).astype(BF16)
    picked = nn(logits.reshape(CTX * HEADS, ROWS).astype(BF16), pick).reshape(CTX, HEADS, ROWS)
    matched = iota((CTX, HEADS, ROWS), 0) == (iota((CTX, HEADS, ROWS), 2) >> 4)
    own_logits = jnp.sum(jnp.where(matched, picked, 0.0), axis=0)
    own_step, own_slope = steps_of(own_logits, bias)
    until = jnp.where(place(lower) <= place(upper), 1.0, 0.0).astype(BF16)
    running = by_mask(speed * own_step, until)
    running_b = by_mask(speed * own_slope, until)
    rows[0] = running
    rows[1] = own_step
    rows[2] = running_b
    rows[3] = own_slope / own_step
    running_c = columns_of(running)
    running_bc = columns_of(running_b)
    for head in range(HEADS):
        rcol[head] = jnp.broadcast_to(running_c[:, head : head + 1], (ROWS, DIM))
        rbcol[head] = jnp.broadcast_to(running_bc[:, head : head + 1], (ROWS, DIM))

    def gathered(piece, batch):
        sources = KEYS // SIZES[piece]
        part = kv[pl.ds(sources * batch, sources), pl.ds(HEAD_ROWS + STARTS[piece], SIZES[piece]), :]
        both = part.reshape(KEYS, 2 * DIM)
        lanes = pl.ds(pl.multiple_of(CTX * STARTS[piece] + batch * KEYS, KEYS), KEYS)
        return both[:, :DIM].astype(F32).T, both[:, DIM:], lanes

    def moments(piece):
        def one(batch):
            key_t, value, lanes = gathered(piece, batch)
            double = twice(value, 0)
            for head in range(HEADS):
                mom[head] += nn(wide(key_t * wts[0, head : head + 1, lanes]), double)

        each(CTX * SIZES[piece] // KEYS, one)

    def tangents(piece):
        def one(batch):
            key_t, value, lanes = gathered(piece, batch)
            for head in range(HEADS):
                by_decay = (key_t * wts[1, head : head + 1, lanes]).astype(BF16)
                by_bias = (key_t * wts[2, head : head + 1, lanes]).astype(BF16)
                tangent[head] += nn(jnp.concatenate([by_decay, by_bias], axis=0), value)

        each(CTX * SIZES[piece] // KEYS, one)

    def sort(piece):
        def one(index):
            block = STARTS[piece] // SUB + index
            part = pl.ds(pl.multiple_of(HEAD_ROWS + SUB * block, SUB), SUB)
            both = kv[:, part, :].reshape(ROWS, 2 * DIM)
            kpos[block] = both[:, :DIM]
            vpos[block, :, :DIM] = both[:, DIM:]
            vpos[block, :, DIM:] = jnp.ones((ROWS, DIM), BF16)

        each(SIZES[piece] // SUB, one)

    def attend(chunk, masked):
        blocks = pl.ds(WIDTH * chunk, WIDTH)
        key = kpos[blocks].reshape(WIDTH * ROWS, DIM)
        value = vpos[blocks].reshape(WIDTH * ROWS, 2 * DIM)

        def mix(head, weights, shrink):
            acc[head] = acc[head] * twice(shrink, 1) + nn(weights, value)

        scores = nt(qh[0], key)
        waiting = None
        for head in range(HEADS):
            following = nt(qh[head + 1], key) if head + 1 < HEADS else None
            if masked:
                scores = scores + hide[...]
            old = top[head]
            new = jnp.maximum(old, jnp.max(scores, axis=1, keepdims=True))
            weights = jnp.exp2((scores - new[:, :1]) * (SCALE * LOG2E)).astype(BF16)
            shrink = jnp.exp2((old - new) * (SCALE * LOG2E))
            top[head] = new
            if waiting is not None:
                mix(*waiting)
            waiting = (head, weights, shrink)
            scores = following
        mix(*waiting)

    sort(0)
    moments(0)
    others(CTX, me, lambda peer: q_copy(peer, peer).wait_recv())
    for head in range(HEADS):
        qh[head] = qr[:, :, head * DIM : (head + 1) * DIM].reshape(ROWS, DIM)

    def teach(chunk, carry):
        attend(chunk, False)

        @pl.when(needs(chip, 1) & (chunk == 0))
        def _():
            relay(1)
            tangents(0)
            arrived(1)
            sort(1)

        @pl.when(needs(chip, 2) & (chunk == 1))
        def _():
            relay(2)
            moments(1)
            arrived(2)
            sort(2)
            moments(2)

        return carry

    lax.fori_loop(0, last, teach, 0)

    @pl.when(needs(chip, 1) & jnp.logical_not(needs(chip, 2)))
    def _():
        moments(1)

    attend(last, True)

    def close(head):
        total = acc[head]
        tq[head] = (total[:, :DIM] / total[:, DIM:]).astype(BF16)

    each(HEADS, close)

    weights[2].wait()
    own_kv = kv[:, pl.ds(pl.multiple_of(HEAD_ROWS + SUB * me, SUB), SUB), :].reshape(ROWS, 2 * DIM)
    kown[...] = twice(own_kv[:, :DIM], 1)
    vown[...] = twice(own_kv[:, DIM:], 1)

    def forward(group):
        heads = [FORWARD * group + index for index in range(FORWARD)]
        read = [halves(nn(qh[h], both_maps[h])) for h in heads]
        score = [nt(wide(r), kown[...]) for r in read]
        causal = place(iota((ROWS, ROWS), 1)) <= place(iota((ROWS, ROWS), 0))
        mixed = []
        for h, r, s in zip(heads, read, score):
            t_all[h] = r
            s_all[h] = s
            gap = twice(rcol[h], 1) - rows[0, pl.ds(h, 1), :]
            decay = jnp.where(causal, jnp.exp(gap), 0.0) * rows[1, pl.ds(h, 1), :]
            d_all[h] = decay
            high, low = split(s * decay)
            value = vown[:, :DIM]
            mixed.append(nn(high, value) + nn(low, value) + jnp.exp(rcol[h]) * product(r, mom[h]))
        flats = [nn(wide(m), twice(x_w[h], 0)) for h, m in zip(heads, mixed)]
        for h, m, flat in zip(heads, mixed, flats):
            z_all[h] = m
            y_all[h] = flat
            taught = tq[h].astype(F32)
            scaled = flat * gains[pl.ds(h, 1), :]
            stats[0] += flat * flat
            stats[1] += taught * taught
            stats[2] += scaled * scaled
            stats[3] += scaled * taught

    each(HEADS // FORWARD, forward)

    line = iota((8, ROWS), 0)
    packed = jnp.zeros((8, ROWS), F32)
    for index in range(4):
        packed = jnp.where(line == index, nt(jnp.ones((8, 2 * DIM), BF16), wide(stats[index])), packed)
    stx[tp] = packed

    def t_copy(peer, slot):
        return remote(stx.at[slot], stx.at[slot], t_ss.at[peer], t_rs.at[slot], {"tp": peer})

    others(TP, tp, lambda peer: t_copy(peer, tp).start())
    for piece in range(PIECES):

        @pl.when(jnp.logical_not(needs(chip, 1)) if piece == 0 else needs(chip, piece))
        def _(piece=piece):
            tangents(piece)

    others(TP, tp, lambda peer: t_copy(peer, peer).wait_recv())
    sums = jnp.sum(stx[...], axis=0)
    inverse = lax.rsqrt(sums[0:1] / FEATURES + EPS)
    inverse_t = lax.rsqrt(sums[1:2] / FEATURES + EPS)
    cross = (2.0 / TOKENS) * (inverse * sums[2:3] - inverse_t * sums[3:4])
    pull = inverse * inverse * inverse * cross / FEATURES
    line = iota((8, ROWS), 0)
    spread = columns_of(jnp.where(line == 0, inverse, jnp.where(line == 1, inverse_t, pull)))
    for index in range(3):
        cols[index] = jnp.broadcast_to(spread[:, index : index + 1], (ROWS, DIM))

    def sib_copy(group):
        part = pl.ds(GROUP * group, GROUP)
        return remote(gbuf.at[1 - core, part], sibr.at[part], sib_ss.at[group], sib_rs.at[group], {"ctx": sibling})

    def r_copy(turn, head, slot):
        return remote(pairsum.at[turn], rs.at[slot], r_ss.at[head], r_rs.at[slot], {"ctx": 2 * head + core})

    def turns(group):
        heads = []
        for index in range(GROUP):
            turn = GROUP * group + index
            owner = (chip + turn) & 3
            first = (owner >> 1) * 5 + (owner & 1) * 2
            heads.append(jnp.where(turn < HEADS // 2, first, first + 1 - 2 * (first & 1)))
        return heads

    def order_of(head):
        if isinstance(head, int):
            return ORDER.index(head)
        late = (head + (head >> 2)) & 1
        return 4 * late + 2 * (head >> 2) + ((head & 3) >> 1)

    def pass_on(group):
        sib_copy(group).wait_recv()
        for index, head in enumerate(turns(group)):
            turn = GROUP * group + index
            both = gbuf[core, turn] + sibr[turn]
            pairsum[turn, :DIM] = both[:DIM].astype(BF16)
            high, low = split(both[DIM:])
            ends = jnp.concatenate([high.astype(F32), low.astype(F32)], axis=0)
            pairsum[turn, DIM:] = ends.astype(BF16)

            @pl.when(head != chip)
            def _(head=head, turn=turn):
                r_copy(turn, head, chip).start()

            @pl.when(head == chip)
            def _(turn=turn):
                rs[chip] = pairsum[turn]

    def backward(group):
        heads = turns(group)
        d_flats, small = [], []
        order = jnp.where(iota((ROWS, ROWS), 0) == place(iota((ROWS, ROWS), 1)), 1.0, 0.0).astype(BF16)
        for h in heads:
            flat = y_all[h]
            gain = gains[pl.ds(h, 1), :]
            inv = cols[0]
            unit = flat * inv
            normed = unit * gain
            out[:, pl.ds(pl.multiple_of(h * DIM, DIM), DIM)] = nn(order, normed.astype(BF16)).astype(BF16)
            d_normed = (2.0 / TOKENS) * (normed - tq[h].astype(F32) * cols[1])
            d_flat = d_normed * gain * inv - flat * cols[2]
            d_flats.append(d_flat)
            moved = d_flat * flat
            small.append([
                jnp.sum(d_normed * unit, axis=0, keepdims=True),
                jnp.sum(moved * rcol[h], axis=0, keepdims=True),
                jnp.sum(moved * rbcol[h], axis=0, keepdims=True),
            ])
        d_mixed = [nt(wide(d), twice(x_w[h], 1)) for h, d in zip(heads, d_flats)]
        d_score = [nt(wide(d), vown[...]) * d_all[h] for h, d in zip(heads, d_mixed)]
        for index, h in enumerate(heads):
            gbuf[1, GROUP * group + index, :DIM] = product(z_all[h].T, d_flats[index])
        d_read = []
        for index, h in enumerate(heads):
            felt = jnp.sum(d_score[index] * s_all[h], axis=0, keepdims=True)
            from_decay = felt * rows[0, pl.ds(h, 1), :]
            from_bias = felt * (rows[3, pl.ds(h, 1), :] - rows[2, pl.ds(h, 1), :])
            high, low = split(d_score[index])
            key = kown[:, :DIM]
            d_late = jnp.exp(rcol[h]) * d_mixed[index]
            d_read.append(nn(high, key) + nn(low, key) + product_t(d_late, mom[h]))
            d_state = product(t_all[h].T, d_late)
            small[index][1] += jnp.sum(d_state * tangent[h, :DIM], axis=0, keepdims=True) - halves(from_decay)
            small[index][2] += jnp.sum(d_state * tangent[h, DIM:], axis=0, keepdims=True) + halves(from_bias)
        tail = iota((TAIL, DIM), 0)
        for index, h in enumerate(heads):
            query_t = qh[h].astype(F32).T.astype(BF16)
            turn = GROUP * group + index
            gbuf[0, turn, :DIM] = halves(nn(query_t, wide(d_read[index])))
            lines = jnp.zeros((TAIL, DIM), F32)
            for line, value in enumerate(small[index]):
                lines = jnp.where(tail == line, value, lines)
            gbuf[0, turn, DIM:] = jnp.zeros((TAIL, DIM), F32)
            gbuf[1, turn, DIM:] = lines
        sib_copy(group).start()

        @pl.when(group > 0)
        def _():
            pass_on(group - 1)

    each(HEADS // GROUP, backward)
    out_copy = pltpu.make_async_copy(out, out_to, out_sem.at[0])
    out_copy.start()
    pass_on(HEADS // GROUP - 1)

    others(CHIPS, chip, lambda peer: r_copy(0, peer, peer).wait_recv())
    whole = jnp.sum(rs[...].astype(F32), axis=0)
    fin[core, order_of(chip), :DIM] = whole[:DIM]
    fin[core, order_of(chip), DIM:] = whole[DIM : DIM + TAIL] + whole[DIM + TAIL :]

    def ag_copy(peer, slot):
        held = fin.at[core, order_of(slot)]
        return remote(held, held, ag_ss.at[peer], ag_rs.at[slot], {"ctx": 2 * peer + core})

    def fw_copy(half, side):
        held = fin.at[side, pl.ds(half * (CHIPS // 2), CHIPS // 2)]
        return remote(held, held, fw_ss.at[half], fw_rs.at[half], {"ctx": sibling})

    def fin_copy(half):
        part = pl.ds(half * (CHIPS // 2), CHIPS // 2)
        return pltpu.make_async_copy(fin.at[:, part], fin_to.at[:, part], fin_sem.at[half])

    others(CHIPS, chip, lambda peer: ag_copy(peer, chip).start())

    others(CTX, me, lambda peer: q_copy(peer, me).wait_send())
    for piece in range(PIECES):

        def left(peer, piece=piece):
            @pl.when(needs(peer, piece))
            def _():
                kv_copy(peer, chip, piece).wait_send()

        others(CHIPS, chip, left)

        @pl.when(needs(chip, piece))
        def _(piece=piece):
            for slot in range(CHIPS):
                kf_copy(slot, core, piece).wait_send()

    others(TP, tp, lambda peer: t_copy(peer, tp).wait_send())
    for half in range(2):
        for head in ORDER[half * (CHIPS // 2) : (half + 1) * (CHIPS // 2)]:

            @pl.when(chip != head)
            def _(head=head):
                ag_copy(head, head).wait_recv()

        fw_copy(half, core).start()
    for half in range(2):
        fw_copy(half, 1 - core).wait_recv()
        fin_copy(half).start()

    others(CHIPS, chip, lambda peer: r_copy(0, peer, chip).wait_send())
    others(CHIPS, chip, lambda peer: ag_copy(peer, chip).wait_send())
    for group in range(HEADS // GROUP):
        sib_copy(group).wait_send()
    for half in range(2):
        fw_copy(half, core).wait_send()
        fin_copy(half).wait()
    out_copy.wait()


def closing(out_in, fin, c_w, b_w, out, grad_c, grad_b, grad_x, grad_decay, grad_bias, grad_gain):
    out[...] = out_in[...]
    for head in range(HEADS):
        slot = ORDER.index(head)
        grad_x[head] = fin[1, slot, :DIM]
        joint = fin[0, slot, :DIM]
        grad_c[head] = nn(wide(joint), twice(b_w[head], 0)) * SCALE
        grad_b[head] = nn(wide(joint.T), twice(c_w[head], 0)) * SCALE
        grad_gain[head * DIM : (head + 1) * DIM] = fin[1, slot, DIM]
        grad_decay[head] = jnp.sum(fin[1, slot, DIM + 1])
        grad_bias[head] = jnp.sum(fin[1, slot, DIM + 2])


def local(queries, keys, values, dt_logits, decay_log, dt_bias, c_weight, b_weight, x_weight, norm_gain):
    whole = pl.BlockSpec(memory_space=pltpu.VMEM)
    there = pl.BlockSpec(memory_space=pl.ANY)
    scalars = pl.BlockSpec(memory_space=pltpu.SMEM)
    dma = pltpu.SemaphoreType.DMA

    def f32(*shape):
        return pltpu.VMEM(shape, F32)

    def bf16(*shape):
        return pltpu.VMEM(shape, BF16)

    square = (HEADS, DIM, DIM)
    by_row = (HEADS, ROWS, DIM)
    message = (DIM + TAIL, DIM)
    short = (DIM + 2 * TAIL, DIM)
    arguments = (
        queries, keys, values, dt_logits.T, decay_log, dt_bias, c_weight, b_weight, x_weight, norm_gain,
    )
    given = [pltpu.with_memory_space_constraint(a, pltpu.HBM) for a in arguments]
    out, fin = pl.pallas_call(
        kernel,
        out_shape=(
            jax.ShapeDtypeStruct((ROWS, HEADS * DIM), BF16),
            jax.ShapeDtypeStruct((2, HEADS, *message), F32),
        ),
        in_specs=[pl.BlockSpec(memory_space=pltpu.HBM)] * 10,
        out_specs=[there] * 2,
        scratch_shapes=[
            bf16(CTX, SUB, HEADS * DIM),
            bf16(CTX, HEAD_ROWS + ROWS, 2 * DIM),
            bf16(CTX, ROWS, DIM),
            bf16(CTX, ROWS, 2 * DIM),
            bf16(*by_row),
            f32(ROWS, WIDTH * ROWS),
            f32(HEADS, ROWS, 2 * DIM),
            f32(*by_row),
            bf16(*by_row),
            f32(*square),
            f32(HEADS, 2 * DIM, DIM),
            f32(3, HEADS, CTX * ROWS),
            f32(4, HEADS, ROWS),
            f32(*by_row),
            f32(*by_row),
            bf16(ROWS, 2 * DIM),
            bf16(ROWS, 2 * DIM),
            f32(HEADS, DIM),
            bf16(HEADS, DIM, 2 * DIM),
            bf16(*square),
            bf16(*square),
            bf16(*square),
            f32(*by_row),
            f32(HEADS, ROWS, ROWS),
            f32(HEADS, ROWS, ROWS),
            f32(*by_row),
            f32(*by_row),
            f32(4, ROWS, DIM),
            f32(TP, 8, ROWS),
            f32(3, ROWS, DIM),
            bf16(ROWS, HEADS * DIM),
            f32(2, HEADS, *message),
            f32(HEADS, *message),
            bf16(HEADS, *short),
            bf16(CHIPS, *short),
            f32(2, HEADS, *message),
            bf16(HEADS, ROWS),
            pltpu.SMEM((HEADS,), F32),
            pltpu.SMEM((HEADS,), F32),
            f32(HEADS * DIM),
            dma((7,)), dma((3,)), dma((1,)), dma((2,)),
            dma((CTX,)), dma((CTX,)),
            dma((CHIPS, PIECES)), dma((CHIPS, PIECES)), dma((CHIPS, PIECES)), dma((CHIPS, PIECES)),
            dma((TP,)), dma((TP,)),
            dma((HEADS // GROUP,)), dma((HEADS // GROUP,)), dma((CHIPS,)), dma((CHIPS,)),
            dma((CHIPS,)), dma((CHIPS,)), dma((2,)), dma((2,)),
        ],
        compiler_params=pltpu.CompilerParams(
            collective_id=0, has_side_effects=True, vmem_limit_bytes=40 * 2**20
        ),
    )(*given)
    return pl.pallas_call(
        closing,
        out_shape=(
            jax.ShapeDtypeStruct((ROWS, HEADS * DIM), BF16),
            jax.ShapeDtypeStruct(square, F32),
            jax.ShapeDtypeStruct(square, F32),
            jax.ShapeDtypeStruct(square, F32),
            jax.ShapeDtypeStruct((HEADS,), F32),
            jax.ShapeDtypeStruct((HEADS,), F32),
            jax.ShapeDtypeStruct((HEADS * DIM,), F32),
        ),
        in_specs=[whole] * 4,
        out_specs=[whole] * 4 + [scalars] * 2 + [whole],
        compiler_params=pltpu.CompilerParams(vmem_limit_bytes=16 * 2**20),
    )(out, fin, c_weight, b_weight)


def solution(mesh):
    return jax.shard_map(
        local,
        mesh=mesh,
        in_specs=(
            P("ctx", "tp"),
            P("ctx", "tp"),
            P("ctx", "tp"),
            P("ctx", "tp"),
            P("tp"),
            P("tp"),
            P("tp", None, None),
            P("tp", None, None),
            P("tp", None, None),
            P("tp"),
        ),
        out_specs=(
            P("ctx", "tp"),
            P("tp", None, None),
            P("tp", None, None),
            P("tp", None, None),
            P("tp"),
            P("tp"),
            P("tp"),
        ),
        check_vma=False,
    )
```

```python
import jax
import jax.numpy as jnp
from jax import lax
from jax.experimental import pallas as pl
from jax.experimental.pallas import tpu as pltpu
from jax.sharding import PartitionSpec as P

MESH = pl.DeviceIdType.MESH
F32 = jnp.float32
BF16 = jnp.bfloat16
HEADS = 8
DIM = 128
ROWS = 256
CTX = 16
TP = 8
CHIPS = CTX // 2
SUB = ROWS // CTX
STARTS = (0, 64, 128)
SIZES = (64, 64, 128)
PIECES = len(STARTS)
WIDTH = 4
KEYS = 512
STACK = 4
HEAD_ROWS = 16
TAIL = 8
GROUP = 2
FORWARD = 4
TOKENS = ROWS * CTX
FEATURES = HEADS * DIM * TP
EPS = 1e-05
SCALE = DIM**-0.5
LOG2E = 1.4426950408889634
NEG = -1e30
ORDER = (0, 2, 5, 7, 1, 3, 4, 6)


def nn(a, b):
    return lax.dot_general(a, b, (((1,), (0,)), ((), ())), preferred_element_type=F32)


def nt(a, b):
    return lax.dot_general(a, b, (((1,), (1,)), ((), ())), preferred_element_type=F32)


def split(value):
    high = value.astype(BF16)
    return high, (value - high.astype(F32)).astype(BF16)


def wide(value):
    return jnp.concatenate(split(value), axis=1)


def twice(value, axis):
    return jnp.concatenate([value, value], axis=axis)


def halves(value):
    return value[:, :DIM] + value[:, DIM:]


def by_mask(value, mask):
    first = value.astype(BF16)
    rest = value - first.astype(F32)
    second = rest.astype(BF16)
    third = (rest - second.astype(F32)).astype(BF16)
    return nn(first, mask) + nn(second, mask) + nn(third, mask)


def product(a, b):
    a_high, a_low = split(a)
    b_high, b_low = split(b)
    return halves(nn(a_high, jnp.concatenate([b_high, b_low], axis=1))) + nn(a_low, b_high)


def left_product(parts, b):
    b_high, b_low = split(b)
    high, low = parts[:, :ROWS], parts[:, ROWS:]
    return halves(nn(high, jnp.concatenate([b_high, b_low], axis=1))) + nn(low, b_high)


def product_t(a, b):
    a_high, a_low = split(a)
    b_high, b_low = split(b)
    return nt(jnp.concatenate([a_high, a_low], axis=1), twice(b_high, 1)) + nt(a_high, b_low)


def iota(shape, axis):
    return lax.broadcasted_iota(jnp.int32, shape, axis)


def place(row):
    return (row & 15) * 16 + (row >> 4)


def columns_of(rows):
    return jnp.concatenate([rows, jnp.zeros((DIM - 8, ROWS), F32)], axis=0).T


def steps_of(logits, bias):
    raised = logits + bias
    faded = jnp.exp(-jnp.abs(raised))
    step = jnp.maximum(raised, 0.0) + jnp.log1p(faded)
    slope = jnp.where(raised >= 0.0, 1.0, faded) / (1.0 + faded)
    return step, slope


def kernel(
    q_in, k_in, v_in, z_hbm, decay_hbm, bias_hbm, c_in, b_in, x_in, gain_hbm,
    out_to, fin_to,
    qr, kv, kpos, vpos, qh, hide, acc, top, tq, mom, tangent, wts, rows, rcol, rbcol, kown, vown, gains, both_maps, faded, zt_all, tt_all, qt_all,
    c_w, b_w, x_w, t_all, s_all, d_all, z_all, y_all, stats, stx, cols, out,
    gbuf, sibr, pairsum, rs, fin,
    z_in, decay_in, bias_in, gain_in,
    local_sem, w_sem, out_sem, fin_sem, q_ss, q_rs, kv_ss, kv_rs, kf_ss, kf_rs, t_ss, t_rs, sib_ss, sib_rs, r_ss, r_rs,
    ag_ss, ag_rs, fw_ss, fw_rs,
):
    me = lax.axis_index("ctx")
    tp = lax.axis_index("tp")
    core = lax.rem(me, 2)
    chip = me // 2
    sibling = me + 1 - 2 * core

    def remote(src, dst, send, recv, where):
        return pltpu.make_async_remote_copy(
            src_ref=src, dst_ref=dst, send_sem=send, recv_sem=recv, device_id=where, device_id_type=MESH
        )

    def others(count, mine, body):
        for step in range(1, count):
            body((mine + step) & (count - 1))

    def each(count, body):
        def one(step, carry):
            body(step)
            return carry

        lax.fori_loop(0, count, one, 0)

    own_rows = pl.ds(pl.multiple_of(SUB * me, SUB), SUB)
    body_rows = pl.ds(HEAD_ROWS, ROWS)
    own = [
        pltpu.make_async_copy(k_in, kv.at[me, body_rows, pl.ds(0, DIM)], local_sem.at[0]),
        pltpu.make_async_copy(v_in, kv.at[me, body_rows, pl.ds(DIM, DIM)], local_sem.at[1]),
        pltpu.make_async_copy(q_in.at[own_rows], qr.at[me], local_sem.at[2]),
    ]
    few = [
        pltpu.make_async_copy(z_hbm, z_in, local_sem.at[3]),
        pltpu.make_async_copy(decay_hbm, decay_in, local_sem.at[4]),
        pltpu.make_async_copy(bias_hbm, bias_in, local_sem.at[5]),
        pltpu.make_async_copy(gain_hbm, gain_in, local_sem.at[6]),
    ]
    for copy in few:
        copy.start()
    for copy in own:
        copy.start()
    weights = [
        pltpu.make_async_copy(c_in, c_w, w_sem.at[0]),
        pltpu.make_async_copy(b_in, b_w, w_sem.at[1]),
        pltpu.make_async_copy(x_in, x_w, w_sem.at[2]),
    ]
    for copy in weights:
        copy.start()
    barrier = pltpu.get_barrier_semaphore()
    others(CTX, me, lambda peer: pl.semaphore_signal(barrier, inc=1, device_id={"ctx": peer}, device_id_type=MESH))
    others(TP, tp, lambda peer: pl.semaphore_signal(barrier, inc=1, device_id={"tp": peer}, device_id_type=MESH))
    for copy in few:
        copy.wait()
    own_z = z_in[...].astype(F32)
    kv[me, :HEAD_ROWS, :] = jnp.concatenate([own_z, jnp.zeros_like(own_z)], axis=0).astype(BF16)
    for head in range(HEADS):
        gains[head : head + 1, :] = gain_in[head * DIM : (head + 1) * DIM].reshape(1, DIM)
        acc[head] = jnp.zeros((ROWS, 2 * DIM), F32)
        top[head] = jnp.full((ROWS, DIM), NEG, F32)
    vpos[:, :, DIM:] = jnp.ones((CTX, ROWS, DIM), BF16)
    mom[...] = jnp.zeros_like(mom)
    tangent[...] = jnp.zeros_like(tangent)
    stats[...] = jnp.zeros_like(stats)
    last = me // WIDTH
    shown = (ROWS, WIDTH * ROWS)
    key_place = place(iota(shown, 1) & (ROWS - 1)) + (iota(shown, 1) >> 8) * ROWS + WIDTH * ROWS * last
    hide[...] = jnp.where(key_place <= place(iota(shown, 0)) + ROWS * me, 0.0, NEG)
    head_line = iota((HEADS, ROWS), 0)
    decay_rate = jnp.zeros((HEADS, ROWS), F32)
    bias = jnp.zeros((HEADS, ROWS), F32)
    for head in range(HEADS):
        decay_rate = jnp.where(head_line == head, decay_in[head], decay_rate)
        bias = jnp.where(head_line == head, bias_in[head], bias)
    speed = -jnp.exp(decay_rate)
    for copy in weights[:2]:
        copy.wait()
    for head in range(HEADS):
        both_maps[head] = wide(nt(c_w[head], b_w[head]) * SCALE)
    for copy in own:
        copy.wait()
    pl.semaphore_wait(barrier, CTX - 1 + TP - 1)

    def part_of(piece):
        if piece == 0:
            return pl.ds(0, HEAD_ROWS + SIZES[0])
        return pl.ds(HEAD_ROWS + STARTS[piece], SIZES[piece])

    def kv_copy(peer, slot, piece):
        held = kv.at[2 * slot + core, part_of(piece)]
        return remote(held, held, kv_ss.at[peer, piece], kv_rs.at[slot, piece], {"ctx": 2 * peer + core})

    def kf_copy(slot, side, piece):
        held = kv.at[2 * slot + side, part_of(piece)]
        return remote(held, held, kf_ss.at[slot, piece], kf_rs.at[slot, piece], {"ctx": sibling})

    def needs(peer, piece):
        return peer >= STARTS[piece] // SUB // 2

    def q_copy(peer, slot):
        taken = pl.ds(pl.multiple_of(SUB * peer, SUB), SUB)
        return remote(q_in.at[taken], qr.at[slot], q_ss.at[peer], q_rs.at[slot], {"ctx": peer})

    def send_piece(piece):
        def send(peer):
            @pl.when(needs(peer, piece))
            def _():
                kv_copy(peer, chip, piece).start()

        others(CHIPS, chip, send)

        @pl.when(needs(chip, piece))
        def _():
            kf_copy(chip, core, piece).start()

    def relay(piece):
        def one(peer):
            kv_copy(peer, peer, piece).wait_recv()
            kf_copy(peer, core, piece).start()

        others(CHIPS, chip, one)

    def arrived(piece):
        kf_copy(chip, 1 - core, piece).wait_recv()
        others(CHIPS, chip, lambda peer: kf_copy(peer, 1 - core, piece).wait_recv())

    send_piece(0)
    others(CTX, me, lambda peer: q_copy(peer, me).start())
    for piece in range(1, PIECES):
        send_piece(piece)

    relay(0)
    arrived(0)

    logits = kv[:, :HEAD_ROWS, :].astype(F32)[:, :HEADS, :]
    step, slope = steps_of(logits, bias[None])
    rate = speed[None] * step
    rate_b = speed[None] * slope
    lower = iota((ROWS, ROWS), 0)
    upper = iota((ROWS, ROWS), 1)
    after = jnp.where((lower > upper) & (lower < SUB * me), 1.0, 0.0).astype(BF16)
    span = by_mask(jnp.sum(rate, axis=0), after)
    span_b = by_mask(jnp.sum(rate_b, axis=0), after)
    earlier = iota((HEADS, ROWS), 1) < SUB * me
    for source in reversed(range(CTX)):
        weight = jnp.where(earlier, jnp.exp(span) * step[source], 0.0)
        kinds = (weight, weight * span, weight * (span_b + slope[source] / step[source]))
        for index, kind in enumerate(kinds):
            for start, size in zip(STARTS, SIZES):
                at = CTX * start + source * size
                wts[index, :, at : at + size] = kind[:, start : start + size]
        span = span + rate[source]
        span_b = span_b + rate_b[source]

    pick = jnp.where(lower == SUB * me + (upper & 15), 1.0, 0.0).astype(BF16)
    picked = nn(logits.reshape(CTX * HEADS, ROWS).astype(BF16), pick).reshape(CTX, HEADS, ROWS)
    matched = iota((CTX, HEADS, ROWS), 0) == (iota((CTX, HEADS, ROWS), 2) >> 4)
    own_logits = jnp.sum(jnp.where(matched, picked, 0.0), axis=0)
    own_step, own_slope = steps_of(own_logits, bias)
    until = jnp.where(place(lower) <= place(upper), 1.0, 0.0).astype(BF16)
    running = by_mask(speed * own_step, until)
    running_b = by_mask(speed * own_slope, until)
    rows[0] = running
    rows[1] = own_step
    rows[2] = running_b
    rows[3] = own_slope / own_step
    running_c = columns_of(running)
    running_bc = columns_of(running_b)
    for head in range(HEADS):
        rcol[head] = jnp.broadcast_to(running_c[:, head : head + 1], (ROWS, DIM))
        rbcol[head] = jnp.broadcast_to(running_bc[:, head : head + 1], (ROWS, DIM))

    def gathered(piece, batch):
        sources = KEYS // SIZES[piece]
        part = kv[pl.ds(sources * batch, sources), pl.ds(HEAD_ROWS + STARTS[piece], SIZES[piece]), :]
        both = part.reshape(KEYS, 2 * DIM)
        lanes = pl.ds(pl.multiple_of(CTX * STARTS[piece] + batch * KEYS, KEYS), KEYS)
        return both[:, :DIM].astype(F32).T, both[:, DIM:], lanes

    def moments(piece):
        def one(batch):
            key_t, value, lanes = gathered(piece, batch)
            for first in range(0, HEADS, STACK):
                parts = []
                for head in range(first, first + STACK):
                    parts.extend(split(key_t * wts[0, head : head + 1, lanes]))
                added = nn(jnp.concatenate(parts, axis=0), value).reshape(STACK, 2, DIM, DIM)
                mom[first : first + STACK] += added[:, 0] + added[:, 1]

        each(CTX * SIZES[piece] // KEYS, one)

    def tangents(piece):
        def one(batch):
            key_t, value, lanes = gathered(piece, batch)
            for first in range(0, HEADS, STACK):
                parts = []
                for head in range(first, first + STACK):
                    parts.append((key_t * wts[1, head : head + 1, lanes]).astype(BF16))
                    parts.append((key_t * wts[2, head : head + 1, lanes]).astype(BF16))
                added = nn(jnp.concatenate(parts, axis=0), value)
                tangent[first : first + STACK] += added.reshape(STACK, 2 * DIM, DIM)

        each(CTX * SIZES[piece] // KEYS, one)

    def sort(piece):
        def one(index):
            block = STARTS[piece] // SUB + index
            part = pl.ds(pl.multiple_of(HEAD_ROWS + SUB * block, SUB), SUB)
            both = kv[:, part, :].reshape(ROWS, 2 * DIM)
            kpos[block] = both[:, :DIM]
            vpos[block, :, :DIM] = both[:, DIM:]

        each(SIZES[piece] // SUB, one)

    def attend(chunk, masked):
        blocks = pl.ds(WIDTH * chunk, WIDTH)
        key = kpos[blocks].reshape(WIDTH * ROWS, DIM)
        value = vpos[blocks].reshape(WIDTH * ROWS, 2 * DIM)

        def mix(head, weights, shrink):
            acc[head] = acc[head] * twice(shrink, 1) + nn(weights, value)

        scores = nt(qh[0], key)
        waiting = None
        for head in range(HEADS):
            following = nt(qh[head + 1], key) if head + 1 < HEADS else None
            if masked:
                scores = scores + hide[...]
            old = top[head]
            new = jnp.maximum(old, jnp.max(scores, axis=1, keepdims=True))
            weights = jnp.exp2((scores - new[:, :1]) * (SCALE * LOG2E)).astype(BF16)
            shrink = jnp.exp2((old - new) * (SCALE * LOG2E))
            top[head] = new
            if waiting is not None:
                mix(*waiting)
            waiting = (head, weights, shrink)
            scores = following
        mix(*waiting)

    sort(0)
    moments(0)
    others(CTX, me, lambda peer: q_copy(peer, peer).wait_recv())
    for head in range(HEADS):
        qh[head] = qr[:, :, head * DIM : (head + 1) * DIM].reshape(ROWS, DIM)

    def teach(chunk, carry):
        attend(chunk, False)

        @pl.when(needs(chip, 1) & (chunk == 0))
        def _():
            relay(1)
            tangents(0)
            arrived(1)
            sort(1)

        @pl.when(needs(chip, 2) & (chunk == 1))
        def _():
            relay(2)
            moments(1)
            arrived(2)
            sort(2)
            moments(2)

        return carry

    lax.fori_loop(0, last, teach, 0)

    @pl.when(needs(chip, 1) & jnp.logical_not(needs(chip, 2)))
    def _():
        moments(1)

    attend(last, True)

    def close(head):
        total = acc[head]
        tq[head] = (total[:, :DIM] / total[:, DIM:]).astype(BF16)

    each(HEADS, close)

    weights[2].wait()
    own_kv = kv[:, pl.ds(pl.multiple_of(HEAD_ROWS + SUB * me, SUB), SUB), :].reshape(ROWS, 2 * DIM)
    kown[...] = twice(own_kv[:, :DIM], 1)
    vown[...] = twice(own_kv[:, DIM:], 1)

    def forward(group):
        heads = [FORWARD * group + index for index in range(FORWARD)]
        read = [halves(nn(qh[h], both_maps[h])) for h in heads]
        score = [nt(wide(r), kown[...]) for r in read]
        causal = place(iota((ROWS, ROWS), 1)) <= place(iota((ROWS, ROWS), 0))
        mixed = []
        for h, r, s in zip(heads, read, score):
            t_all[h] = r
            s_all[h] = s
            gap = twice(rcol[h], 1) - rows[0, pl.ds(h, 1), :]
            decay = jnp.where(causal, jnp.exp(gap), 0.0) * rows[1, pl.ds(h, 1), :]
            d_all[h] = decay
            high, low = split(s * decay)
            value = vown[:, :DIM]
            fade = jnp.exp(rcol[h])
            faded[h] = fade
            mixed.append(nn(high, value) + nn(low, value) + fade * product(r, mom[h]))
        flats = [nn(wide(m), twice(x_w[h], 0)) for h, m in zip(heads, mixed)]
        for h, m, flat in zip(heads, mixed, flats):
            z_all[h] = m
            y_all[h] = flat
            taught = tq[h].astype(F32)
            scaled = flat * gains[pl.ds(h, 1), :]
            stats[0] += flat * flat
            stats[1] += taught * taught
            stats[2] += scaled * scaled
            stats[3] += scaled * taught

    each(HEADS // FORWARD, forward)

    line = iota((8, ROWS), 0)
    packed = jnp.zeros((8, ROWS), F32)
    for index in range(4):
        packed = jnp.where(line == index, nt(jnp.ones((8, 2 * DIM), BF16), wide(stats[index])), packed)
    stx[tp] = packed

    def t_copy(peer, slot):
        return remote(stx.at[slot], stx.at[slot], t_ss.at[peer], t_rs.at[slot], {"tp": peer})

    others(TP, tp, lambda peer: t_copy(peer, tp).start())
    for piece in range(PIECES):

        @pl.when(jnp.logical_not(needs(chip, 1)) if piece == 0 else needs(chip, piece))
        def _(piece=piece):
            tangents(piece)

    def turn_over(head):
        zt_all[head] = wide(z_all[head].T)
        tt_all[head] = wide(t_all[head].T)
        qt_all[head] = qh[head].astype(F32).T.astype(BF16)

    each(HEADS, turn_over)
    others(TP, tp, lambda peer: t_copy(peer, peer).wait_recv())
    sums = jnp.sum(stx[...], axis=0)
    inverse = lax.rsqrt(sums[0:1] / FEATURES + EPS)
    inverse_t = lax.rsqrt(sums[1:2] / FEATURES + EPS)
    cross = (2.0 / TOKENS) * (inverse * sums[2:3] - inverse_t * sums[3:4])
    pull = inverse * inverse * inverse * cross / FEATURES
    line = iota((8, ROWS), 0)
    spread = columns_of(jnp.where(line == 0, inverse, jnp.where(line == 1, inverse_t, pull)))
    for index in range(3):
        cols[index] = jnp.broadcast_to(spread[:, index : index + 1], (ROWS, DIM))

    def sib_copy(group):
        part = pl.ds(GROUP * group, GROUP)
        return remote(gbuf.at[1 - core, part], sibr.at[part], sib_ss.at[group], sib_rs.at[group], {"ctx": sibling})

    def r_copy(turn, head, slot):
        return remote(pairsum.at[turn], rs.at[slot], r_ss.at[head], r_rs.at[slot], {"ctx": 2 * head + core})

    def turns(group):
        heads = []
        for index in range(GROUP):
            turn = GROUP * group + index
            owner = (chip + turn) & 3
            first = (owner >> 1) * 5 + (owner & 1) * 2
            heads.append(jnp.where(turn < HEADS // 2, first, first + 1 - 2 * (first & 1)))
        return heads

    def order_of(head):
        if isinstance(head, int):
            return ORDER.index(head)
        late = (head + (head >> 2)) & 1
        return 4 * late + 2 * (head >> 2) + ((head & 3) >> 1)

    def pass_on(group):
        sib_copy(group).wait_recv()
        for index, head in enumerate(turns(group)):
            turn = GROUP * group + index
            both = gbuf[core, turn] + sibr[turn]
            pairsum[turn, :DIM] = both[:DIM].astype(BF16)
            high, low = split(both[DIM:])
            ends = jnp.concatenate([high.astype(F32), low.astype(F32)], axis=0)
            pairsum[turn, DIM:] = ends.astype(BF16)

            @pl.when(head != chip)
            def _(head=head, turn=turn):
                r_copy(turn, head, chip).start()

            @pl.when(head == chip)
            def _(turn=turn):
                rs[chip] = pairsum[turn]

    def backward(group):
        heads = turns(group)
        d_flats, small = [], []
        for h in heads:
            flat = y_all[h]
            gain = gains[pl.ds(h, 1), :]
            inv = cols[0]
            unit = flat * inv
            normed = unit * gain
            d_normed = (2.0 / TOKENS) * (normed - tq[h].astype(F32) * cols[1])
            d_flat = d_normed * gain * inv - flat * cols[2]
            d_flats.append(d_flat)
            moved = d_flat * flat
            small.append([
                jnp.sum(d_normed * unit, axis=0, keepdims=True),
                jnp.sum(moved * rcol[h], axis=0, keepdims=True),
                jnp.sum(moved * rbcol[h], axis=0, keepdims=True),
            ])
        d_mixed = [nt(wide(d), twice(x_w[h], 1)) for h, d in zip(heads, d_flats)]
        d_score = [nt(wide(d), vown[...]) * d_all[h] for h, d in zip(heads, d_mixed)]
        for index, h in enumerate(heads):
            gbuf[1, GROUP * group + index, :DIM] = left_product(zt_all[h], d_flats[index])
        d_read = []
        for index, h in enumerate(heads):
            felt = jnp.sum(d_score[index] * s_all[h], axis=0, keepdims=True)
            from_decay = felt * rows[0, pl.ds(h, 1), :]
            from_bias = felt * (rows[3, pl.ds(h, 1), :] - rows[2, pl.ds(h, 1), :])
            high, low = split(d_score[index])
            key = kown[:, :DIM]
            d_late = faded[h] * d_mixed[index]
            d_read.append(nn(high, key) + nn(low, key) + product_t(d_late, mom[h]))
            d_state = left_product(tt_all[h], d_late)
            small[index][1] += jnp.sum(d_state * tangent[h, :DIM], axis=0, keepdims=True) - halves(from_decay)
            small[index][2] += jnp.sum(d_state * tangent[h, DIM:], axis=0, keepdims=True) + halves(from_bias)
        tail = iota((TAIL, DIM), 0)
        for index, h in enumerate(heads):
            turn = GROUP * group + index
            gbuf[0, turn, :DIM] = halves(nn(qt_all[h], wide(d_read[index])))
            lines = jnp.zeros((TAIL, DIM), F32)
            for line, value in enumerate(small[index]):
                lines = jnp.where(tail == line, value, lines)
            gbuf[0, turn, DIM:] = jnp.zeros((TAIL, DIM), F32)
            gbuf[1, turn, DIM:] = lines
        sib_copy(group).start()

        @pl.when(group > 0)
        def _():
            pass_on(group - 1)

    each(HEADS // GROUP, backward)
    pass_on(HEADS // GROUP - 1)

    others(CHIPS, chip, lambda peer: r_copy(0, peer, peer).wait_recv())
    whole = jnp.sum(rs[...].astype(F32), axis=0)
    fin[core, order_of(chip), :DIM] = whole[:DIM]
    fin[core, order_of(chip), DIM:] = whole[DIM : DIM + TAIL] + whole[DIM + TAIL :]

    def ag_copy(peer, slot):
        held = fin.at[core, order_of(slot)]
        return remote(held, held, ag_ss.at[peer], ag_rs.at[slot], {"ctx": 2 * peer + core})

    def fw_copy(half, side):
        held = fin.at[side, pl.ds(half * (CHIPS // 2), CHIPS // 2)]
        return remote(held, held, fw_ss.at[half], fw_rs.at[half], {"ctx": sibling})

    def fin_copy(half):
        part = pl.ds(half * (CHIPS // 2), CHIPS // 2)
        return pltpu.make_async_copy(fin.at[:, part], fin_to.at[:, part], fin_sem.at[half])

    others(CHIPS, chip, lambda peer: ag_copy(peer, chip).start())

    order = jnp.where(iota((ROWS, ROWS), 0) == place(iota((ROWS, ROWS), 1)), 1.0, 0.0).astype(BF16)
    for head in range(HEADS):
        normed = y_all[head] * cols[0] * gains[head : head + 1, :]
        out[:, head * DIM : (head + 1) * DIM] = nn(order, normed.astype(BF16)).astype(BF16)
    out_copy = pltpu.make_async_copy(out, out_to, out_sem.at[0])
    out_copy.start()

    others(CTX, me, lambda peer: q_copy(peer, me).wait_send())
    for piece in range(PIECES):

        def left(peer, piece=piece):
            @pl.when(needs(peer, piece))
            def _():
                kv_copy(peer, chip, piece).wait_send()

        others(CHIPS, chip, left)

        @pl.when(needs(chip, piece))
        def _(piece=piece):
            for slot in range(CHIPS):
                kf_copy(slot, core, piece).wait_send()

    others(TP, tp, lambda peer: t_copy(peer, tp).wait_send())
    for half in range(2):
        for head in ORDER[half * (CHIPS // 2) : (half + 1) * (CHIPS // 2)]:

            @pl.when(chip != head)
            def _(head=head):
                ag_copy(head, head).wait_recv()

        fw_copy(half, core).start()
    for half in range(2):
        fw_copy(half, 1 - core).wait_recv()
        fin_copy(half).start()

    others(CHIPS, chip, lambda peer: r_copy(0, peer, chip).wait_send())
    others(CHIPS, chip, lambda peer: ag_copy(peer, chip).wait_send())
    for group in range(HEADS // GROUP):
        sib_copy(group).wait_send()
    for half in range(2):
        fw_copy(half, core).wait_send()
        fin_copy(half).wait()
    out_copy.wait()


def closing(out_in, fin, c_w, b_w, out, grad_c, grad_b, grad_x, grad_decay, grad_bias, grad_gain):
    out[...] = out_in[...]
    for head in range(HEADS):
        slot = ORDER.index(head)
        grad_x[head] = fin[1, slot, :DIM]
        joint = fin[0, slot, :DIM]
        grad_c[head] = nn(wide(joint), twice(b_w[head], 0)) * SCALE
        grad_b[head] = nn(wide(joint.T), twice(c_w[head], 0)) * SCALE
        grad_gain[head * DIM : (head + 1) * DIM] = fin[1, slot, DIM]
        grad_decay[head] = jnp.sum(fin[1, slot, DIM + 1])
        grad_bias[head] = jnp.sum(fin[1, slot, DIM + 2])


def local(queries, keys, values, dt_logits, decay_log, dt_bias, c_weight, b_weight, x_weight, norm_gain):
    whole = pl.BlockSpec(memory_space=pltpu.VMEM)
    there = pl.BlockSpec(memory_space=pl.ANY)
    scalars = pl.BlockSpec(memory_space=pltpu.SMEM)
    dma = pltpu.SemaphoreType.DMA

    def f32(*shape):
        return pltpu.VMEM(shape, F32)

    def bf16(*shape):
        return pltpu.VMEM(shape, BF16)

    square = (HEADS, DIM, DIM)
    by_row = (HEADS, ROWS, DIM)
    message = (DIM + TAIL, DIM)
    short = (DIM + 2 * TAIL, DIM)
    arguments = (
        queries, keys, values, dt_logits.T, decay_log, dt_bias, c_weight, b_weight, x_weight, norm_gain,
    )
    given = [pltpu.with_memory_space_constraint(a, pltpu.HBM) for a in arguments]
    out, fin = pl.pallas_call(
        kernel,
        out_shape=(
            jax.ShapeDtypeStruct((ROWS, HEADS * DIM), BF16),
            jax.ShapeDtypeStruct((2, HEADS, *message), F32),
        ),
        in_specs=[pl.BlockSpec(memory_space=pltpu.HBM)] * 10,
        out_specs=[there] * 2,
        scratch_shapes=[
            bf16(CTX, SUB, HEADS * DIM),
            bf16(CTX, HEAD_ROWS + ROWS, 2 * DIM),
            bf16(CTX, ROWS, DIM),
            bf16(CTX, ROWS, 2 * DIM),
            bf16(*by_row),
            f32(ROWS, WIDTH * ROWS),
            f32(HEADS, ROWS, 2 * DIM),
            f32(*by_row),
            bf16(*by_row),
            f32(*square),
            f32(HEADS, 2 * DIM, DIM),
            f32(3, HEADS, CTX * ROWS),
            f32(4, HEADS, ROWS),
            f32(*by_row),
            f32(*by_row),
            bf16(ROWS, 2 * DIM),
            bf16(ROWS, 2 * DIM),
            f32(HEADS, DIM),
            bf16(HEADS, DIM, 2 * DIM),
            f32(*by_row),
            bf16(HEADS, DIM, 2 * ROWS),
            bf16(HEADS, DIM, 2 * ROWS),
            bf16(HEADS, DIM, ROWS),
            bf16(*square),
            bf16(*square),
            bf16(*square),
            f32(*by_row),
            f32(HEADS, ROWS, ROWS),
            f32(HEADS, ROWS, ROWS),
            f32(*by_row),
            f32(*by_row),
            f32(4, ROWS, DIM),
            f32(TP, 8, ROWS),
            f32(3, ROWS, DIM),
            bf16(ROWS, HEADS * DIM),
            f32(2, HEADS, *message),
            f32(HEADS, *message),
            bf16(HEADS, *short),
            bf16(CHIPS, *short),
            f32(2, HEADS, *message),
            bf16(HEADS, ROWS),
            pltpu.SMEM((HEADS,), F32),
            pltpu.SMEM((HEADS,), F32),
            f32(HEADS * DIM),
            dma((7,)), dma((3,)), dma((1,)), dma((2,)),
            dma((CTX,)), dma((CTX,)),
            dma((CHIPS, PIECES)), dma((CHIPS, PIECES)), dma((CHIPS, PIECES)), dma((CHIPS, PIECES)),
            dma((TP,)), dma((TP,)),
            dma((HEADS // GROUP,)), dma((HEADS // GROUP,)), dma((CHIPS,)), dma((CHIPS,)),
            dma((CHIPS,)), dma((CHIPS,)), dma((2,)), dma((2,)),
        ],
        compiler_params=pltpu.CompilerParams(
            collective_id=0, has_side_effects=True, vmem_limit_bytes=40 * 2**20
        ),
    )(*given)
    return pl.pallas_call(
        closing,
        out_shape=(
            jax.ShapeDtypeStruct((ROWS, HEADS * DIM), BF16),
            jax.ShapeDtypeStruct(square, F32),
            jax.ShapeDtypeStruct(square, F32),
            jax.ShapeDtypeStruct(square, F32),
            jax.ShapeDtypeStruct((HEADS,), F32),
            jax.ShapeDtypeStruct((HEADS,), F32),
            jax.ShapeDtypeStruct((HEADS * DIM,), F32),
        ),
        in_specs=[whole] * 4,
        out_specs=[whole] * 4 + [scalars] * 2 + [whole],
        compiler_params=pltpu.CompilerParams(vmem_limit_bytes=16 * 2**20),
    )(out, fin, c_weight, b_weight)


def solution(mesh):
    return jax.shard_map(
        local,
        mesh=mesh,
        in_specs=(
            P("ctx", "tp"),
            P("ctx", "tp"),
            P("ctx", "tp"),
            P("ctx", "tp"),
            P("tp"),
            P("tp"),
            P("tp", None, None),
            P("tp", None, None),
            P("tp", None, None),
            P("tp"),
        ),
        out_specs=(
            P("ctx", "tp"),
            P("tp", None, None),
            P("tp", None, None),
            P("tp", None, None),
            P("tp"),
            P("tp"),
            P("tp"),
        ),
        check_vma=False,
    )
```
